256 devices in a mesh: fiber: 64 (over z, y_lo, x), seg: 4 (over y_hi, core).
Axes of the slice: x: 4, y: 4 (y_hi: 2, y_lo: 2; y = y_hi * 2 + y_lo), z: 8, core: 2. Of those that a mesh axis runs over, the one named last changes fastest.
Arguments:
- raw_strain: bfloat16 [64, 8192, 2048], P('seg', 'fiber'), may hold values from -6 to 6
- fir_taps: float32 [31], replicated, may hold values from -1 to 1
- good_mask: int32 [64, 8192], P('seg', 'fiber'), may hold values from 0 to 1, as said below
Outputs:
- stacked_spectra: float32 [144, 8192, 2, 128], P('seg', 'fiber')
The draws below stay inside these ranges and needn't reach their ends.
Inputs may be any that keep to these rules, and one draw needn't show every extreme that they name: `good_mask`: 0 or 1; some channels are 0 in every segment.
All inputs are finite; a program needn't handle non-finite values.
Results may differ from the reference program's by a relative error of at most 0.005.
Values may be sent and summed in bfloat16 or wider, within the bound.
No kernel may reach another device: no remote copies, remote signals or barrier semaphores. Data moves between devices by JAX's collectives and lax.ppermute only.
A program may use at most 192 MiB of HBM per device.

```python
import math
import jax
import jax.numpy as jnp
from jax import lax

SAMPLES = 2048
NF = 144
LOW = 16
HALF = 15
TAPS = 31
SMOOTH = 4
LAGS = 128
CH_DEV = 128
NCH = 8192
SEGS = 64


def draw_good_mask(key, part):
    key_dead = jax.random.fold_in(key, 11)
    key_drop = jax.random.fold_in(key, 12)
    alive = jax.random.randint(key_dead, (1, NCH), 0, 16) != 0
    kept = jax.random.randint(key_drop, (SEGS, NCH), 0, 5) != 0
    return (alive & kept).astype(jnp.int32)


def block_levels(key, shape, pieces, least, largest):
    level, own = 1.0, jax.random.fold_in(key, 6)
    for axis_at, parts in pieces:
        draws = jnp.exp(jax.random.uniform(jax.random.fold_in(own, axis_at), (parts,), jnp.float32, least / len(pieces), largest / len(pieces)))
        level = level * jnp.repeat(draws, shape[axis_at] // parts).reshape([-1 if axis == axis_at else 1 for axis in range(len(shape))])
    return level


def gaussian(rng, shape, scale, limit, split=(), held_as=jnp.bfloat16):
    loudness = block_levels(rng, shape, split, -0.22, 0.18) if split else 1.0
    values = jax.random.normal(rng, shape, jnp.float32) * scale * loudness
    return jnp.minimum(jnp.maximum(values, -limit), limit).astype(held_as)


def setup_inputs(seed: int = 0) -> dict:
    seeds = jax.random.split(jax.random.key(seed), 4)
    return {
        "raw_strain": gaussian(seeds[0], (SEGS, NCH, SAMPLES), 1.0, 6.0, ((0, 4), (1, 64))),
        "fir_taps": jnp.clip(jax.random.uniform(seeds[1], (TAPS,), jnp.float32, -1.0, 1.0), -1.0, 1.0),
        "good_mask": draw_good_mask(jax.random.fold_in(seeds[3], 71), 0),
    }


epsilon = 1e-06
water_share = 0.1

def dft_basis(samples):
    times = jnp.arange(samples, dtype=jnp.int32)
    bins = jnp.arange(NF, dtype=jnp.int32) + LOW
    phase_index = times[:, None] * bins[None, :] % samples
    angles = phase_index.astype(jnp.float32) * (2.0 * math.pi / samples)
    return jnp.stack([jnp.cos(angles), -jnp.sin(angles)], axis=2).astype(jnp.bfloat16)

def lag_band(gram):
    lead = gram.shape[:-2]
    rows = gram.shape[-2]
    cols = gram.shape[-1]
    flat = gram.reshape(lead + (rows * cols,))
    padding = [(0, 0)] * len(lead) + [(0, rows)]
    flat = jnp.pad(flat, padding)
    skewed = flat.reshape(lead + (rows, cols + 1))
    return skewed[..., 1:1 + LAGS]

def whiten(filtered, good_mask):
    powers = filtered[:, :, 0] * filtered[:, :, 0] + filtered[:, :, 1] * filtered[:, :, 1]
    bin_count = powers.shape[1]
    padded = jnp.pad(powers, ((0, 0), (SMOOTH, SMOOTH), (0, 0)))
    smooth = padded[:, 0:bin_count]
    for offset in range(1, 2 * SMOOTH + 1):
        smooth = smooth + padded[:, offset:offset + bin_count]
    smooth = smooth / (2 * SMOOTH + 1)
    water_level = lax.optimization_barrier(jnp.mean(powers, axis=1, keepdims=True))
    divisor = jnp.sqrt(smooth + water_share * water_level + epsilon)
    scaled = good_mask.astype(jnp.float32)[:, None, :] / divisor
    return (filtered * scaled[:, :, None, :]).astype(jnp.bfloat16)

def cross_band(left_block, extended):
    rotated = jnp.stack([extended[:, :, 1], -extended[:, :, 0]], axis=2)
    gram_real = jnp.einsum('sfrc,sfrd->fcd', left_block, extended, precision=lax.Precision.HIGHEST)
    gram_imag = jnp.einsum('sfrc,sfrd->fcd', left_block, rotated, precision=lax.Precision.HIGHEST)
    return jnp.stack([lag_band(gram_real), lag_band(gram_imag)], axis=2)

def reference(raw_strain, fir_taps, good_mask):
    basis = dft_basis(SAMPLES).astype(jnp.float32)

    def one_segment(inputs):
        segment, segment_mask = inputs
        spectra = jnp.einsum('ct,tfr->frc', segment.astype(jnp.float32), basis, precision=lax.Precision.HIGHEST)
        padded = jnp.pad(spectra, ((0, 0), (0, 0), (HALF, HALF)))
        filtered = fir_taps[0] * padded[:, :, 0:NCH]
        for tap_index in range(1, 2 * HALF + 1):
            filtered = filtered + fir_taps[tap_index] * padded[:, :, tap_index:tap_index + NCH]
        return whiten(filtered[None], segment_mask[None])[0]
    whitened = lax.map(one_segment, (raw_strain, good_mask))
    padded_white = jnp.pad(whitened, ((0, 0), (0, 0), (0, 0), (0, CH_DEV)))
    mask_float = good_mask.astype(jnp.float32)
    padded_mask = jnp.pad(mask_float, ((0, 0), (0, CH_DEV)))

    def one_block(block_index):
        first = (block_index * CH_DEV).astype(jnp.int32)
        left_block = lax.dynamic_slice_in_dim(whitened, first, CH_DEV, 3).astype(jnp.float32)
        extended = lax.dynamic_slice_in_dim(padded_white, first, 2 * CH_DEV, 3).astype(jnp.float32)
        sums = cross_band(left_block, extended)
        mask_left = lax.dynamic_slice_in_dim(mask_float, first, CH_DEV, 1)
        mask_wide = lax.dynamic_slice_in_dim(padded_mask, first, 2 * CH_DEV, 1)
        counts = lag_band(jnp.einsum('sc,sd->cd', mask_left, mask_wide, precision=lax.Precision.HIGHEST))
        return sums / jnp.maximum(counts, 1.0)[None, :, None, :]
    blocks = lax.map(one_block, jnp.arange(NCH // CH_DEV, dtype=jnp.int32))
    return jnp.transpose(blocks, (1, 0, 2, 3, 4)).reshape(NF, NCH, 2, LAGS)
```

```python
import functools
import math

import jax
import jax.numpy as jnp
import numpy as np
from jax import lax
from jax.experimental import pallas as pl
from jax.experimental.pallas import tpu as pltpu
from jax.sharding import PartitionSpec as P

NF = 144
LOW = 16
SMOOTH = 4
LAGS = 128
EDGE = 16
HALF = 15

epsilon = 1e-06
water_share = 0.1

GRID = ("fiber", "seg")
VMEM = 56 * 1024 * 1024
F32 = jnp.float32
BF16 = jnp.bfloat16


def basis_rows(samples):
    times = np.arange(samples, dtype=np.int64)
    bins = np.arange(NF, dtype=np.int64) + LOW
    phase_index = bins[:, None] * times[None, :] % samples
    angles = phase_index.astype(np.float32) * np.float32(2.0 * math.pi / samples)
    rows = np.concatenate([np.cos(angles), -np.sin(angles)], axis=0)
    return jnp.asarray(rows, dtype=BF16)


def filter_band(taps, count, first, shape):
    offset = lax.broadcasted_iota(jnp.int32, shape, 0) - lax.broadcasted_iota(jnp.int32, shape, 1)
    band = jnp.zeros(shape, F32)
    for tap in range(count):
        band = jnp.where(offset == tap - first - HALF, taps[tap], band)
    return band


NT = (((1,), (1,)), ((), ()))
TN = (((0,), (0,)), ((), ()))


def dot(a, b, dims=(((1,), (0,)), ((), ()))):
    return lax.dot_general(a, b, dims, preferred_element_type=F32)


def edge_kernel(basis, first, last, head, tail):
    rows = first.shape[0] * EDGE
    samples = first.shape[2]
    head[...] = dot(basis[...], first[...].reshape(rows, samples), NT).astype(BF16)
    tail[...] = dot(basis[...], last[...].reshape(rows, samples), NT).astype(BF16)


def edge_spectra(basis, raw):
    segs, channels, samples = raw.shape
    out = jax.ShapeDtypeStruct((2 * NF, segs * EDGE), BF16)
    return pl.pallas_call(
        edge_kernel,
        grid=(1,),
        in_specs=[
            pl.BlockSpec(basis.shape, lambda i: (0, 0)),
            pl.BlockSpec((segs, EDGE, samples), lambda i: (0, 0, 0)),
            pl.BlockSpec((segs, EDGE, samples), lambda i: (0, channels // EDGE - 1, 0)),
        ],
        out_specs=[pl.BlockSpec(out.shape, lambda i: (0, 0))] * 2,
        out_shape=[out, out],
        compiler_params=pltpu.CompilerParams(vmem_limit_bytes=VMEM),
        name="edge_spectra",
    )(basis, raw, raw)


def main_kernel(segs, count, basis, raw, taps, filtered, high, low):
    step = pl.program_id(0)

    @pl.when(step == 0)
    def _():
        band = filter_band(taps, count, 0, high.shape)
        high[...] = band.astype(BF16)
        low[...] = (band - high[...].astype(F32)).astype(BF16)

    pair, channels, samples = raw.shape
    spectra = dot(basis[...], raw[...].reshape(pair * channels, samples), NT)
    for at in range(pair):
        part = spectra[:, at * channels : (at + 1) * channels]
        top = part.astype(BF16)
        rest = (part - top.astype(F32)).astype(BF16)
        sums = dot(top, high[...]) + dot(rest, high[...]) + dot(top, low[...])
        filtered[pl.ds(step * pair + at, 2 * NF, stride=segs), :] = sums


def main_spectra(basis, raw, taps):
    segs, channels, samples = raw.shape
    pair = 2
    return pl.pallas_call(
        functools.partial(main_kernel, segs, taps.shape[0]),
        grid=(segs // pair,),
        in_specs=[
            pl.BlockSpec(basis.shape, lambda i: (0, 0)),
            pl.BlockSpec((pair, channels, samples), lambda i: (i, 0, 0)),
            pl.BlockSpec(memory_space=pltpu.SMEM),
        ],
        out_specs=pl.BlockSpec((2 * NF * segs, channels), lambda i: (0, 0)),
        out_shape=jax.ShapeDtypeStruct((2 * NF * segs, channels), F32),
        scratch_shapes=[pltpu.VMEM((channels, channels), BF16)] * 2,
        compiler_params=pltpu.CompilerParams(vmem_limit_bytes=VMEM),
        name="main_spectra",
    )(basis, raw, taps)


def whiten_kernel(parts, count, me, taps, filtered, left, right, mask, *refs):
    outs, (total, powers) = refs[:parts], refs[parts:]
    segs, channels = mask.shape
    rows = segs * EDGE
    share = NF // parts
    owner = lax.broadcasted_iota(jnp.int32, (rows, channels), 0) // EDGE
    band_left = filter_band(taps, count, -EDGE, (EDGE, channels))
    band_right = filter_band(taps, count, channels, (EDGE, channels))
    wide_left = jnp.concatenate([band_left] * segs, axis=0)
    wide_right = jnp.concatenate([band_right] * segs, axis=0)
    for seg in range(segs):
        here = owner == seg
        sums = dot(left[...], jnp.where(here, wide_left, 0.0).astype(BF16))
        sums += dot(right[...], jnp.where(here, wide_right, 0.0).astype(BF16))
        at = pl.ds(seg, 2 * NF, stride=segs)
        total[at, :] = sums
    powers[0:SMOOTH] = jnp.zeros((SMOOTH, segs, channels), F32)
    powers[SMOOTH + NF :] = jnp.zeros((SMOOTH, segs, channels), F32)
    block = 12

    def square(step, water):
        first = pl.multiple_of(step * (block * segs), segs)
        second = pl.multiple_of(first + NF * segs, segs)
        real = total[pl.ds(first, block * segs), :] + filtered[pl.ds(first, block * segs), :]
        imag = total[pl.ds(second, block * segs), :] + filtered[pl.ds(second, block * segs), :]
        total[pl.ds(first, block * segs), :] = real
        total[pl.ds(second, block * segs), :] = imag
        power = (real * real + imag * imag).reshape(block, segs, channels)
        powers[pl.ds(step * block + SMOOTH, block)] = power
        return water + power.sum(0)

    water = lax.fori_loop(0, NF // block, square, jnp.zeros((segs, channels), F32))
    floor = water * (water_share / NF) + epsilon
    good = mask[...].astype(F32)
    for k in range(parts):
        start = (me[0] ^ k) * share
        out = outs[k]

        def spread(step, carry, start=start, out=out):
            bin_at = start + step * block
            cells = powers[pl.ds(bin_at, block + 2 * SMOOTH)]
            two = cells[:-1] + cells[1:]
            four = two[:-2] + two[2:]
            eight = four[:-4] + four[4:]
            nine = eight[:block] + cells[2 * SMOOTH :]
            scaled = good * lax.rsqrt(nine * (1.0 / (2 * SMOOTH + 1)) + floor)
            first = pl.multiple_of(bin_at * segs, segs)
            second = pl.multiple_of(first + NF * segs, segs)
            real = total[pl.ds(first, block * segs), :].reshape(block, segs, channels) * scaled
            imag = total[pl.ds(second, block * segs), :].reshape(block, segs, channels) * scaled
            both = jnp.concatenate([real[:, None], imag[:, None]], axis=1).astype(BF16)
            at = pl.multiple_of(step * (block * 2 * segs), segs)
            out[pl.ds(at, block * 2 * segs), :] = both.reshape(block * 2 * segs, channels)
            return carry

        lax.fori_loop(0, share // block, spread, 0)
        out[share * 2 * segs :, :] = good.astype(BF16)


def whitened_parts(parts, me, taps, filtered, left, right, mask):
    segs, channels = mask.shape
    rows = NF // parts * 2 * segs + segs
    whole = pl.BlockSpec(memory_space=pltpu.VMEM)
    return pl.pallas_call(
        functools.partial(whiten_kernel, parts, taps.shape[0]),
        in_specs=[pl.BlockSpec(memory_space=pltpu.SMEM)] * 2 + [whole] * 4,
        out_specs=[whole] * parts,
        out_shape=[jax.ShapeDtypeStruct((rows, channels), BF16)] * parts,
        scratch_shapes=[
            pltpu.VMEM((2 * NF * segs, channels), F32),
            pltpu.VMEM((NF + 2 * SMOOTH, segs, channels), F32),
        ],
        compiler_params=pltpu.CompilerParams(vmem_limit_bytes=VMEM),
        name="whiten",
    )(me, taps, filtered, left, right, mask)


def gram_kernel(parts, segs, bins, *refs):
    own, later, own_mask, later_mask = (refs[i * parts : (i + 1) * parts] for i in range(4))
    out, scale = refs[4 * parts :]
    channels = own[0].shape[1]
    row = lax.broadcasted_iota(jnp.int32, (channels, channels), 0)
    column = lax.broadcasted_iota(jnp.int32, (channels, channels), 1)
    ahead = column > row
    skew = (row + column + 1) % channels

    @pl.when(pl.program_id(0) == 0)
    def _():
        mine = jnp.concatenate([ref[...] for ref in own_mask], axis=0)
        theirs = jnp.concatenate([ref[...] for ref in later_mask], axis=0)
        count = jnp.where(ahead, dot(mine, mine, TN), dot(mine, theirs, TN))
        scale[...] = 1.0 / jnp.maximum(count, 1.0)

    for at in range(bins):
        here = [ref[at * 2 * segs : (at + 1) * 2 * segs, :] for ref in own]
        mine = jnp.concatenate(here, axis=0)
        turned = jnp.concatenate(
            [piece for cells in here for piece in (-cells[segs:], cells[:segs])], axis=0
        )
        theirs = jnp.concatenate(
            [ref[at * 2 * segs : (at + 1) * 2 * segs, :] for ref in later], axis=0
        )
        gram = dot(
            jnp.concatenate([mine, turned], axis=1), jnp.concatenate([mine, theirs], axis=1), TN
        )
        for part in range(2):
            rows = gram[part * channels : (part + 1) * channels]
            band = jnp.where(ahead, rows[:, :channels], rows[:, channels:]) * scale[...]
            band = jnp.take_along_axis(band, skew, axis=1, mode="promise_in_bounds")
            out[at, pl.ds(part, channels, stride=2), :] = band


def stacked(parts, segs, own, later):
    channels = own[0].shape[1]
    share = NF // parts
    bins = 4
    cells = pl.BlockSpec((bins * 2 * segs, channels), lambda i: (i, 0))
    flags = pl.BlockSpec((segs, channels), lambda i: (share * 2, 0))
    return pl.pallas_call(
        functools.partial(gram_kernel, parts, segs, bins),
        grid=(share // bins,),
        in_specs=[cells] * (2 * parts) + [flags] * (2 * parts),
        out_specs=pl.BlockSpec((bins, 2 * channels, LAGS), lambda i: (i, 0, 0)),
        out_shape=jax.ShapeDtypeStruct((share, 2 * channels, LAGS), F32),
        scratch_shapes=[pltpu.VMEM((channels, channels), F32)],
        compiler_params=pltpu.CompilerParams(vmem_limit_bytes=VMEM),
        name="gram",
    )(*own, *later, *own, *later)


def on_device(fibers, parts, raw_strain, fir_taps, good_mask):
    segs, channels, samples = raw_strain.shape
    basis = basis_rows(samples)
    me = lax.axis_index("seg").astype(jnp.int32)
    head, tail = edge_spectra(basis, raw_strain)
    left = lax.ppermute(tail, "fiber", [(i, i + 1) for i in range(fibers - 1)])
    right = lax.ppermute(head, "fiber", [(i + 1, i) for i in range(fibers - 1)])
    filtered = main_spectra(basis, raw_strain, fir_taps)
    mine = whitened_parts(parts, me[None], fir_taps, filtered, left, right, good_mask)
    own = [mine[0]]
    for k in range(1, parts):
        own.append(lax.ppermute(mine[k], "seg", [(i, i ^ k) for i in range(parts)]))
    later = [
        lax.ppermute(cells, "fiber", [(i + 1, i) for i in range(fibers - 1)]) for cells in own
    ]
    out = stacked(parts, segs, own, later)
    return out.reshape(out.shape[0], channels, 2, LAGS)


def solution(mesh):
    return jax.shard_map(
        functools.partial(on_device, mesh.shape["fiber"], mesh.shape["seg"]),
        mesh=mesh,
        in_specs=(P("seg", "fiber", None), P(), P("seg", "fiber")),
        out_specs=P("seg", "fiber", None, None),
        check_vma=False,
    )
```

```python
import functools
import math

import jax
import jax.numpy as jnp
import numpy as np
from jax import lax
from jax.experimental import pallas as pl
from jax.experimental.pallas import tpu as pltpu
from jax.sharding import PartitionSpec as P

NF = 144
LOW = 16
SMOOTH = 4
LAGS = 128
EDGE = 16
HALF = 15

epsilon = 1e-06
water_share = 0.1

GRID = ("fiber", "seg")
VMEM = 56 * 1024 * 1024
F32 = jnp.float32
BF16 = jnp.bfloat16


def basis_rows(samples):
    times = np.arange(samples, dtype=np.int64)
    bins = np.arange(NF, dtype=np.int64) + LOW
    phase_index = bins[:, None] * times[None, :] % samples
    angles = phase_index.astype(np.float32) * np.float32(2.0 * math.pi / samples)
    rows = np.concatenate([np.cos(angles), -np.sin(angles)], axis=0)
    return jnp.asarray(rows, dtype=BF16)


def filter_band(taps, count, first, shape):
    offset = lax.broadcasted_iota(jnp.int32, shape, 0) - lax.broadcasted_iota(jnp.int32, shape, 1)
    band = jnp.zeros(shape, F32)
    for tap in range(count):
        band = jnp.where(offset == tap - first - HALF, taps[tap], band)
    return band


NT = (((1,), (1,)), ((), ()))
TN = (((0,), (0,)), ((), ()))


def dot(a, b, dims=(((1,), (0,)), ((), ()))):
    return lax.dot_general(a, b, dims, preferred_element_type=F32)


def edge_kernel(basis, first, last, head, tail):
    rows = first.shape[0] * EDGE
    samples = first.shape[2]
    head[...] = dot(basis[...], first[...].reshape(rows, samples), NT).astype(BF16)
    tail[...] = dot(basis[...], last[...].reshape(rows, samples), NT).astype(BF16)


def edge_spectra(basis, raw):
    segs, channels, samples = raw.shape
    out = jax.ShapeDtypeStruct((2 * NF, segs * EDGE), BF16)
    return pl.pallas_call(
        edge_kernel,
        grid=(1,),
        in_specs=[
            pl.BlockSpec(basis.shape, lambda i: (0, 0)),
            pl.BlockSpec((segs, EDGE, samples), lambda i: (0, 0, 0)),
            pl.BlockSpec((segs, EDGE, samples), lambda i: (0, channels // EDGE - 1, 0)),
        ],
        out_specs=[pl.BlockSpec(out.shape, lambda i: (0, 0))] * 2,
        out_shape=[out, out],
        compiler_params=pltpu.CompilerParams(vmem_limit_bytes=VMEM),
        name="edge_spectra",
    )(basis, raw, raw)


def main_kernel(segs, count, basis, raw, taps, filtered, both):
    step = pl.program_id(0)
    pair, channels, samples = raw.shape

    @pl.when(step == 0)
    def _():
        band = filter_band(taps, count, 0, (channels, channels))
        high = band.astype(BF16)
        low = (band - high.astype(F32)).astype(BF16)
        both[...] = jnp.concatenate(
            [
                jnp.concatenate([high, low], axis=1),
                jnp.concatenate([high, jnp.zeros_like(high)], axis=1),
            ],
            axis=0,
        )

    spectra = dot(basis[...], raw[...].reshape(pair * channels, samples), NT)
    for at in range(pair):
        part = spectra[:, at * channels : (at + 1) * channels]
        top = part.astype(BF16)
        rest = (part - top.astype(F32)).astype(BF16)
        sums = dot(jnp.concatenate([top, rest], axis=1), both[...])
        sums = sums[:, :channels] + sums[:, channels:]
        filtered[pl.ds(step * pair + at, 2 * NF, stride=segs), :] = sums


def main_spectra(basis, raw, taps):
    segs, channels, samples = raw.shape
    pair = 2
    return pl.pallas_call(
        functools.partial(main_kernel, segs, taps.shape[0]),
        grid=(segs // pair,),
        in_specs=[
            pl.BlockSpec(basis.shape, lambda i: (0, 0)),
            pl.BlockSpec((pair, channels, samples), lambda i: (i, 0, 0)),
            pl.BlockSpec(memory_space=pltpu.SMEM),
        ],
        out_specs=pl.BlockSpec((2 * NF * segs, channels), lambda i: (0, 0)),
        out_shape=jax.ShapeDtypeStruct((2 * NF * segs, channels), F32),
        scratch_shapes=[pltpu.VMEM((2 * channels, 2 * channels), BF16)],
        compiler_params=pltpu.CompilerParams(vmem_limit_bytes=VMEM),
        name="main_spectra",
    )(basis, raw, taps)


def whiten_kernel(parts, count, me, taps, filtered, left, right, mask, *refs):
    outs, (total, powers) = refs[:parts], refs[parts:]
    segs, channels = mask.shape
    rows = segs * EDGE
    share = NF // parts
    owner = lax.broadcasted_iota(jnp.int32, (rows, channels), 0) // EDGE
    band_left = filter_band(taps, count, -EDGE, (EDGE, channels))
    band_right = filter_band(taps, count, channels, (EDGE, channels))
    wide_left = jnp.concatenate([band_left] * segs, axis=0)
    wide_right = jnp.concatenate([band_right] * segs, axis=0)
    for seg in range(segs):
        here = owner == seg
        sums = dot(left[...], jnp.where(here, wide_left, 0.0).astype(BF16))
        sums += dot(right[...], jnp.where(here, wide_right, 0.0).astype(BF16))
        at = pl.ds(seg, 2 * NF, stride=segs)
        total[at, :] = sums
    powers[0:SMOOTH] = jnp.zeros((SMOOTH, segs, channels), F32)
    powers[SMOOTH + NF :] = jnp.zeros((SMOOTH, segs, channels), F32)
    block = 12

    def square(step, water):
        first = pl.multiple_of(step * (block * segs), segs)
        second = pl.multiple_of(first + NF * segs, segs)
        real = total[pl.ds(first, block * segs), :] + filtered[pl.ds(first, block * segs), :]
        imag = total[pl.ds(second, block * segs), :] + filtered[pl.ds(second, block * segs), :]
        total[pl.ds(first, block * segs), :] = real
        total[pl.ds(second, block * segs), :] = imag
        power = (real * real + imag * imag).reshape(block, segs, channels)
        powers[pl.ds(step * block + SMOOTH, block)] = power
        return water + power.sum(0)

    water = lax.fori_loop(0, NF // block, square, jnp.zeros((segs, channels), F32))
    floor = water * (water_share / NF) + epsilon
    good = mask[...].astype(F32)
    for k in range(parts):
        start = (me[0] ^ k) * share
        out = outs[k]

        def spread(step, carry, start=start, out=out):
            bin_at = start + step * block
            cells = powers[pl.ds(bin_at, block + 2 * SMOOTH)]
            two = cells[:-1] + cells[1:]
            four = two[:-2] + two[2:]
            eight = four[:-4] + four[4:]
            nine = eight[:block] + cells[2 * SMOOTH :]
            scaled = good * lax.rsqrt(nine * (1.0 / (2 * SMOOTH + 1)) + floor)
            first = pl.multiple_of(bin_at * segs, segs)
            second = pl.multiple_of(first + NF * segs, segs)
            real = total[pl.ds(first, block * segs), :].reshape(block, segs, channels) * scaled
            imag = total[pl.ds(second, block * segs), :].reshape(block, segs, channels) * scaled
            both = jnp.concatenate([real[:, None], imag[:, None]], axis=1).astype(BF16)
            at = pl.multiple_of(step * (block * 2 * segs), segs)
            out[pl.ds(at, block * 2 * segs), :] = both.reshape(block * 2 * segs, channels)
            return carry

        lax.fori_loop(0, share // block, spread, 0)
        out[share * 2 * segs :, :] = good.astype(BF16)


def whitened_parts(parts, me, taps, filtered, left, right, mask):
    segs, channels = mask.shape
    rows = NF // parts * 2 * segs + segs
    whole = pl.BlockSpec(memory_space=pltpu.VMEM)
    return pl.pallas_call(
        functools.partial(whiten_kernel, parts, taps.shape[0]),
        in_specs=[pl.BlockSpec(memory_space=pltpu.SMEM)] * 2 + [whole] * 4,
        out_specs=[whole] * parts,
        out_shape=[jax.ShapeDtypeStruct((rows, channels), BF16)] * parts,
        scratch_shapes=[
            pltpu.VMEM((2 * NF * segs, channels), F32),
            pltpu.VMEM((NF + 2 * SMOOTH, segs, channels), F32),
        ],
        compiler_params=pltpu.CompilerParams(vmem_limit_bytes=VMEM),
        name="whiten",
    )(me, taps, filtered, left, right, mask)


def gram_kernel(parts, segs, bins, *refs):
    own, later, own_mask, later_mask = (refs[i * parts : (i + 1) * parts] for i in range(4))
    out, scale = refs[4 * parts :]
    channels = own[0].shape[1]
    row = lax.broadcasted_iota(jnp.int32, (channels, channels), 0)
    column = lax.broadcasted_iota(jnp.int32, (channels, channels), 1)
    ahead = column > row
    skew = (row + column + 1) % channels

    @pl.when(pl.program_id(0) == 0)
    def _():
        mine = jnp.concatenate([ref[...] for ref in own_mask], axis=0)
        theirs = jnp.concatenate([ref[...] for ref in later_mask], axis=0)
        count = jnp.where(ahead, dot(mine, mine, TN), dot(mine, theirs, TN))
        scale[...] = 1.0 / jnp.maximum(count, 1.0)

    for at in range(bins):
        here = [ref[at * 2 * segs : (at + 1) * 2 * segs, :] for ref in own]
        mine = jnp.concatenate(here, axis=0)
        turned = jnp.concatenate(
            [piece for cells in here for piece in (-cells[segs:], cells[:segs])], axis=0
        )
        theirs = jnp.concatenate(
            [ref[at * 2 * segs : (at + 1) * 2 * segs, :] for ref in later], axis=0
        )
        gram = dot(
            jnp.concatenate([mine, turned], axis=1), jnp.concatenate([mine, theirs], axis=1), TN
        )
        for part in range(2):
            rows = gram[part * channels : (part + 1) * channels]
            band = jnp.where(ahead, rows[:, :channels], rows[:, channels:]) * scale[...]
            band = jnp.take_along_axis(band, skew, axis=1, mode="promise_in_bounds")
            out[at, pl.ds(part, channels, stride=2), :] = band


def stacked(parts, segs, own, later):
    channels = own[0].shape[1]
    share = NF // parts
    bins = 4
    cells = pl.BlockSpec((bins * 2 * segs, channels), lambda i: (i, 0))
    flags = pl.BlockSpec((segs, channels), lambda i: (share * 2, 0))
    return pl.pallas_call(
        functools.partial(gram_kernel, parts, segs, bins),
        grid=(share // bins,),
        in_specs=[cells] * (2 * parts) + [flags] * (2 * parts),
        out_specs=pl.BlockSpec((bins, 2 * channels, LAGS), lambda i: (i, 0, 0)),
        out_shape=jax.ShapeDtypeStruct((share, 2 * channels, LAGS), F32),
        scratch_shapes=[pltpu.VMEM((channels, channels), F32)],
        compiler_params=pltpu.CompilerParams(vmem_limit_bytes=VMEM),
        name="gram",
    )(*own, *later, *own, *later)


def on_device(fibers, parts, raw_strain, fir_taps, good_mask):
    segs, channels, samples = raw_strain.shape
    basis = basis_rows(samples)
    me = lax.axis_index("seg").astype(jnp.int32)
    head, tail = edge_spectra(basis, raw_strain)
    left = lax.ppermute(tail, "fiber", [(i, i + 1) for i in range(fibers - 1)])
    right = lax.ppermute(head, "fiber", [(i + 1, i) for i in range(fibers - 1)])
    filtered = main_spectra(basis, raw_strain, fir_taps)
    mine = whitened_parts(parts, me[None], fir_taps, filtered, left, right, good_mask)
    own = [mine[0]]
    for k in range(1, parts):
        own.append(lax.ppermute(mine[k], "seg", [(i, i ^ k) for i in range(parts)]))
    later = []
    for k in range(parts):
        pairs = [
            ((i + 1) * parts + (j ^ k), i * parts + j)
            for i in range(fibers - 1)
            for j in range(parts)
        ]
        later.append(lax.ppermute(mine[k], GRID, pairs))
    out = stacked(parts, segs, own, later)
    return out.reshape(out.shape[0], channels, 2, LAGS)


def solution(mesh):
    return jax.shard_map(
        functools.partial(on_device, mesh.shape["fiber"], mesh.shape["seg"]),
        mesh=mesh,
        in_specs=(P("seg", "fiber", None), P(), P("seg", "fiber")),
        out_specs=P("seg", "fiber", None, None),
        check_vma=False,
    )
```

```python
import functools
import math

import jax
import jax.numpy as jnp
import numpy as np
from jax import lax
from jax.experimental import pallas as pl
from jax.experimental.pallas import tpu as pltpu
from jax.sharding import PartitionSpec as P

NF = 144
LOW = 16
SMOOTH = 4
LAGS = 128
EDGE = 16
HALF = 15

epsilon = 1e-06
water_share = 0.1

GRID = ("fiber", "seg")
VMEM = 24 * 1024 * 1024
STREAM = 50 * 1024 * 1024
F32 = jnp.float32
BF16 = jnp.bfloat16


def basis_rows(samples):
    times = np.arange(samples, dtype=np.int64)
    bins = np.arange(NF, dtype=np.int64) + LOW
    phase_index = bins[:, None] * times[None, :] % samples
    angles = phase_index.astype(np.float32) * np.float32(2.0 * math.pi / samples)
    rows = np.concatenate([np.cos(angles), -np.sin(angles)], axis=0)
    return jnp.asarray(rows, dtype=BF16)


def filter_band(taps, count, first, shape):
    offset = lax.broadcasted_iota(jnp.int32, shape, 0) - lax.broadcasted_iota(jnp.int32, shape, 1)
    band = jnp.zeros(shape, F32)
    for tap in range(count):
        band = jnp.where(offset == tap - first - HALF, taps[tap], band)
    return band


NT = (((1,), (1,)), ((), ()))
TN = (((0,), (0,)), ((), ()))


def dot(a, b, dims=(((1,), (0,)), ((), ()))):
    return lax.dot_general(a, b, dims, preferred_element_type=F32)


WHOLE = pl.BlockSpec(memory_space=pltpu.VMEM)
SCALARS = pl.BlockSpec(memory_space=pltpu.SMEM)
ANYWHERE = pl.BlockSpec(memory_space=pl.ANY)


def edge_kernel(raw, basis, head, tail, cells, sems):
    segs, channels, samples = raw.shape
    copies = [
        pltpu.make_async_copy(raw.at[:, pl.ds(first, EDGE), :], cells.at[at], sems.at[at])
        for at, first in enumerate((channels - EDGE, 0))
    ]
    for copy in copies:
        copy.start()
    for at, out in enumerate((tail, head)):
        copies[at].wait()
        out[...] = dot(basis[...], cells[at].reshape(segs * EDGE, samples), NT).astype(BF16)


def edge_spectra(basis, raw):
    segs, channels, samples = raw.shape
    out = jax.ShapeDtypeStruct((2 * NF, segs * EDGE), BF16)
    return pl.pallas_call(
        edge_kernel,
        in_specs=[ANYWHERE, WHOLE],
        out_specs=[WHOLE] * 2,
        out_shape=[out, out],
        scratch_shapes=[
            pltpu.VMEM((2, segs, EDGE, samples), BF16),
            pltpu.SemaphoreType.DMA((2,)),
        ],
        compiler_params=pltpu.CompilerParams(vmem_limit_bytes=STREAM),
        name="edge_spectra",
    )(raw, basis)


def main_kernel(pair, count, raw, basis, taps, filtered, cells, both, sems):
    segs, channels, samples = raw.shape
    copies = [
        pltpu.make_async_copy(
            raw.at[pl.ds(at * pair, pair)], cells.at[pl.ds(at * pair, pair)], sems.at[at]
        )
        for at in range(segs // pair)
    ]
    for copy in copies:
        copy.start()
    band = filter_band(taps, count, 0, (channels, channels))
    high = band.astype(BF16)
    low = (band - high.astype(F32)).astype(BF16)
    both[...] = jnp.concatenate(
        [
            jnp.concatenate([high, low], axis=1),
            jnp.concatenate([high, jnp.zeros_like(high)], axis=1),
        ],
        axis=0,
    )
    for step in range(segs // pair):
        copies[step].wait()
        block = cells[step * pair : (step + 1) * pair].reshape(pair * channels, samples)
        spectra = dot(basis[...], block, NT)
        for at in range(pair):
            part = spectra[:, at * channels : (at + 1) * channels]
            top = part.astype(BF16)
            rest = (part - top.astype(F32)).astype(BF16)
            sums = dot(jnp.concatenate([top, rest], axis=1), both[...])
            sums = sums[:, :channels] + sums[:, channels:]
            filtered[pl.ds(step * pair + at, 2 * NF, stride=segs), :] = sums


def main_spectra(basis, raw, taps):
    segs, channels, samples = raw.shape
    pair = 2
    return pl.pallas_call(
        functools.partial(main_kernel, pair, taps.shape[0]),
        in_specs=[ANYWHERE, WHOLE, SCALARS],
        out_specs=WHOLE,
        out_shape=jax.ShapeDtypeStruct((2 * NF * segs, channels), F32),
        scratch_shapes=[
            pltpu.VMEM((segs, channels, samples), BF16),
            pltpu.VMEM((2 * channels, 2 * channels), BF16),
            pltpu.SemaphoreType.DMA((segs // pair,)),
        ],
        compiler_params=pltpu.CompilerParams(vmem_limit_bytes=STREAM),
        name="main_spectra",
    )(raw, basis, taps)


def whiten_kernel(parts, count, me, taps, filtered, left, right, mask, *refs):
    near, far, other, total, powers = refs
    segs, channels = mask.shape
    height = near.shape[0]
    places = [(near, 0), (other, 0), (far, 0), (other, height)]
    rows = segs * EDGE
    share = NF // parts
    owner = lax.broadcasted_iota(jnp.int32, (rows, channels), 0) // EDGE
    band_left = filter_band(taps, count, -EDGE, (EDGE, channels))
    band_right = filter_band(taps, count, channels, (EDGE, channels))
    wide_left = jnp.concatenate([band_left] * segs, axis=0)
    wide_right = jnp.concatenate([band_right] * segs, axis=0)
    for seg in range(segs):
        here = owner == seg
        sums = dot(left[...], jnp.where(here, wide_left, 0.0).astype(BF16))
        sums += dot(right[...], jnp.where(here, wide_right, 0.0).astype(BF16))
        at = pl.ds(seg, 2 * NF, stride=segs)
        total[at, :] = sums
    powers[0:SMOOTH] = jnp.zeros((SMOOTH, segs, channels), F32)
    powers[SMOOTH + NF :] = jnp.zeros((SMOOTH, segs, channels), F32)
    block = 12

    def square(step, water):
        first = pl.multiple_of(step * (block * segs), segs)
        second = pl.multiple_of(first + NF * segs, segs)
        real = total[pl.ds(first, block * segs), :] + filtered[pl.ds(first, block * segs), :]
        imag = total[pl.ds(second, block * segs), :] + filtered[pl.ds(second, block * segs), :]
        total[pl.ds(first, block * segs), :] = real
        total[pl.ds(second, block * segs), :] = imag
        power = (real * real + imag * imag).reshape(block, segs, channels)
        powers[pl.ds(step * block + SMOOTH, block)] = power
        return water + power.sum(0)

    water = lax.fori_loop(0, NF // block, square, jnp.zeros((segs, channels), F32))
    floor = water * (water_share / NF) + epsilon
    good = mask[...].astype(F32)
    for k in range(parts):
        start = (me[0] ^ k) * share
        out, base = places[k]

        def spread(step, carry, start=start, out=out, base=base):
            bin_at = start + step * block
            cells = powers[pl.ds(bin_at, block + 2 * SMOOTH)]
            two = cells[:-1] + cells[1:]
            four = two[:-2] + two[2:]
            eight = four[:-4] + four[4:]
            nine = eight[:block] + cells[2 * SMOOTH :]
            scaled = good * lax.rsqrt(nine * (1.0 / (2 * SMOOTH + 1)) + floor)
            first = pl.multiple_of(bin_at * segs, segs)
            second = pl.multiple_of(first + NF * segs, segs)
            real = total[pl.ds(first, block * segs), :].reshape(block, segs, channels) * scaled
            imag = total[pl.ds(second, block * segs), :].reshape(block, segs, channels) * scaled
            both = jnp.concatenate([real[:, None], imag[:, None]], axis=1).astype(BF16)
            at = pl.multiple_of(base + step * (block * 2 * segs), segs)
            out[pl.ds(at, block * 2 * segs), :] = both.reshape(block * 2 * segs, channels)
            return carry

        lax.fori_loop(0, share // block, spread, 0)
        out[base + share * 2 * segs : base + height, :] = good.astype(BF16)


def whitened_parts(parts, me, taps, filtered, left, right, mask):
    segs, channels = mask.shape
    rows = NF // parts * 2 * segs + segs
    return pl.pallas_call(
        functools.partial(whiten_kernel, parts, taps.shape[0]),
        in_specs=[SCALARS] * 2 + [WHOLE] * 4,
        out_specs=[WHOLE] * 3,
        out_shape=[jax.ShapeDtypeStruct((height, channels), BF16) for height in (rows, rows, 2 * rows)],
        scratch_shapes=[
            pltpu.VMEM((2 * NF * segs, channels), F32),
            pltpu.VMEM((NF + 2 * SMOOTH, segs, channels), F32),
        ],
        compiler_params=pltpu.CompilerParams(vmem_limit_bytes=VMEM),
        name="whiten",
    )(me, taps, filtered, left, right, mask)


def gram_kernel(segs, bins, *refs):
    own, later, (out, cells, sems) = refs[:2], refs[2:4], refs[4:]
    channels = own[0].shape[1]
    height = own[0].shape[0] // 2
    share = out.shape[0]
    row = lax.broadcasted_iota(jnp.int32, (channels, channels), 0)
    column = lax.broadcasted_iota(jnp.int32, (channels, channels), 1)
    ahead = column > row
    skew = (row + column + 1) % channels
    offsets = [(ref, base) for ref in range(2) for base in (0, height)]

    def pieces(side, first, size):
        return [side[ref][pl.ds(base + first, size), :] for ref, base in offsets]

    mine = jnp.concatenate(pieces(own, height - segs, segs), axis=0)
    theirs = jnp.concatenate(pieces(later, height - segs, segs), axis=0)
    count = jnp.where(ahead, dot(mine, mine, TN), dot(mine, theirs, TN))
    scale = 1.0 / jnp.maximum(count, 1.0)

    def group(step, carry):
        for at in range(bins):
            bin_at = step * bins + at
            first = pl.multiple_of(bin_at * (2 * segs), 2 * segs)
            here = pieces(own, first, 2 * segs)
            mine = jnp.concatenate(here, axis=0)
            turned = jnp.concatenate(
                [piece for part in here for piece in (-part[segs:], part[:segs])], axis=0
            )
            theirs = jnp.concatenate(pieces(later, first, 2 * segs), axis=0)
            gram = dot(
                jnp.concatenate([mine, turned], axis=1), jnp.concatenate([mine, theirs], axis=1), TN
            )
            for part in range(2):
                rows = gram[part * channels : (part + 1) * channels]
                band = jnp.where(ahead, rows[:, :channels], rows[:, channels:]) * scale
                band = jnp.take_along_axis(band, skew, axis=1, mode="promise_in_bounds")
                cells[bin_at, pl.ds(part, channels, stride=2), :] = band
        at = pl.ds(step * bins, bins)
        pltpu.make_async_copy(cells.at[at], out.at[at], sems.at[step]).start()
        return carry

    lax.fori_loop(0, share // bins, group, 0)
    for step in range(share // bins):
        at = pl.ds(step * bins, bins)
        pltpu.make_async_copy(cells.at[at], out.at[at], sems.at[step]).wait()


def stacked(parts, segs, own, later):
    channels = own[0].shape[1]
    share = NF // parts
    bins = 4
    shape = (share, 2 * channels, LAGS)
    return pl.pallas_call(
        functools.partial(gram_kernel, segs, bins),
        in_specs=[WHOLE] * 4,
        out_specs=ANYWHERE,
        out_shape=jax.ShapeDtypeStruct(shape, F32),
        scratch_shapes=[pltpu.VMEM(shape, F32), pltpu.SemaphoreType.DMA((share // bins,))],
        compiler_params=pltpu.CompilerParams(vmem_limit_bytes=VMEM),
        name="gram",
    )(*own, *later)


def on_device(fibers, parts, raw_strain, fir_taps, good_mask):
    segs, channels, samples = raw_strain.shape
    basis = basis_rows(samples)
    me = lax.axis_index("seg").astype(jnp.int32)
    head, tail = edge_spectra(basis, raw_strain)
    left = lax.ppermute(tail, "fiber", [(i, i + 1) for i in range(fibers - 1)])
    right = lax.ppermute(head, "fiber", [(i + 1, i) for i in range(fibers - 1)])
    filtered = main_spectra(basis, raw_strain, fir_taps)
    near, far, other = whitened_parts(
        parts, me[None], fir_taps, filtered, left, right, good_mask
    )
    rows = near.shape[0]
    swapped = lax.ppermute(other, "seg", [(j, j ^ 1) for j in range(parts)])
    near = jnp.concatenate([near, swapped[:rows]], axis=0)
    far = jnp.concatenate([far, swapped[rows:]], axis=0)

    def following(cells, flip):
        pairs = [
            ((i + 1) * parts + (j ^ flip), i * parts + j)
            for i in range(fibers - 1)
            for j in range(parts)
        ]
        return lax.ppermute(cells, GRID, pairs)

    later_far = following(far, 2)
    own_far = lax.ppermute(far, "seg", [(j, j ^ 2) for j in range(parts)])
    later_near = following(near, 0)
    out = stacked(parts, segs, (near, own_far), (later_near, later_far))
    return out.reshape(out.shape[0], channels, 2, LAGS)


def solution(mesh):
    return jax.shard_map(
        functools.partial(on_device, mesh.shape["fiber"], mesh.shape["seg"]),
        mesh=mesh,
        in_specs=(P("seg", "fiber", None), P(), P("seg", "fiber")),
        out_specs=P("seg", "fiber", None, None),
        check_vma=False,
    )
```

```python
import functools
import math

import jax
import jax.numpy as jnp
import numpy as np
from jax import lax
from jax.experimental import pallas as pl
from jax.experimental.pallas import tpu as pltpu
from jax.sharding import PartitionSpec as P

NF = 144
LOW = 16
SMOOTH = 4
LAGS = 128
EDGE = 16
HALF = 15

epsilon = 1e-06
water_share = 0.1

GRID = ("fiber", "seg")
VMEM = 24 * 1024 * 1024
STREAM = 50 * 1024 * 1024
F32 = jnp.float32
BF16 = jnp.bfloat16


def basis_rows(samples):
    times = np.arange(samples, dtype=np.int64)
    bins = np.arange(NF, dtype=np.int64) + LOW
    phase_index = bins[:, None] * times[None, :] % samples
    angles = phase_index.astype(np.float32) * np.float32(2.0 * math.pi / samples)
    rows = np.concatenate([np.cos(angles), -np.sin(angles)], axis=0)
    return jnp.asarray(rows, dtype=BF16)


def filter_band(taps, count, first, shape):
    offset = lax.broadcasted_iota(jnp.int32, shape, 0) - lax.broadcasted_iota(jnp.int32, shape, 1)
    band = jnp.zeros(shape, F32)
    for tap in range(count):
        band = jnp.where(offset == tap - first - HALF, taps[tap], band)
    return band


NT = (((1,), (1,)), ((), ()))
TN = (((0,), (0,)), ((), ()))


def dot(a, b, dims=(((1,), (0,)), ((), ()))):
    return lax.dot_general(a, b, dims, preferred_element_type=F32)


WHOLE = pl.BlockSpec(memory_space=pltpu.VMEM)
SCALARS = pl.BlockSpec(memory_space=pltpu.SMEM)
ANYWHERE = pl.BlockSpec(memory_space=pl.ANY)


def edge_kernel(first, last, basis, head, tail):
    for cells, out in ((last, tail), (first, head)):
        segs, width, samples = cells.shape
        out[...] = dot(basis[...], cells[...].reshape(segs * width, samples), NT).astype(BF16)


def edge_spectra(basis, raw):
    segs, channels, samples = raw.shape
    out = jax.ShapeDtypeStruct((2 * NF, segs * EDGE), BF16)
    return pl.pallas_call(
        edge_kernel,
        in_specs=[WHOLE] * 3,
        out_specs=[WHOLE] * 2,
        out_shape=[out, out],
        compiler_params=pltpu.CompilerParams(vmem_limit_bytes=VMEM),
        name="edge_spectra",
    )(raw[:, :EDGE], raw[:, channels - EDGE :], basis)


def main_kernel(pair, count, raw, basis, taps, filtered, both):
    segs, channels, samples = raw.shape
    band = filter_band(taps, count, 0, (channels, channels))
    high = band.astype(BF16)
    low = (band - high.astype(F32)).astype(BF16)
    both[...] = jnp.concatenate(
        [
            jnp.concatenate([high, low], axis=1),
            jnp.concatenate([high, jnp.zeros_like(high)], axis=1),
        ],
        axis=0,
    )
    for step in range(segs // pair):
        block = raw[step * pair : (step + 1) * pair].reshape(pair * channels, samples)
        spectra = dot(basis[...], block, NT)
        for at in range(pair):
            part = spectra[:, at * channels : (at + 1) * channels]
            top = part.astype(BF16)
            rest = (part - top.astype(F32)).astype(BF16)
            sums = dot(jnp.concatenate([top, rest], axis=1), both[...])
            sums = sums[:, :channels] + sums[:, channels:]
            filtered[pl.ds(step * pair + at, 2 * NF, stride=segs), :] = sums


def main_spectra(basis, raw, taps):
    segs, channels, samples = raw.shape
    return pl.pallas_call(
        functools.partial(main_kernel, 4, taps.shape[0]),
        in_specs=[WHOLE, WHOLE, SCALARS],
        out_specs=WHOLE,
        out_shape=jax.ShapeDtypeStruct((2 * NF * segs, channels), F32),
        scratch_shapes=[pltpu.VMEM((2 * channels, 2 * channels), BF16)],
        compiler_params=pltpu.CompilerParams(vmem_limit_bytes=VMEM),
        name="main_spectra",
    )(raw, basis, taps)


def whiten_kernel(parts, count, me, taps, filtered, left, right, mask, *refs):
    near, far, other, total, powers = refs
    segs, channels = powers.shape[1:]
    height = near.shape[0]
    places = [(near, 0), (other, 0), (far, 0), (other, height)]
    share = NF // parts
    width = segs * EDGE
    owner = lax.broadcasted_iota(jnp.int32, (2 * width, channels), 0) // EDGE % segs
    wide = jnp.concatenate(
        [filter_band(taps, count, -EDGE, (EDGE, channels))] * segs
        + [filter_band(taps, count, channels, (EDGE, channels))] * segs,
        axis=0,
    )
    sides = jnp.concatenate([left[...], right[...]], axis=1)
    for seg in range(segs):
        at = pl.ds(seg, 2 * NF, stride=segs)
        total[at, :] = dot(sides, jnp.where(owner == seg, wide, 0.0).astype(BF16))
    powers[0:SMOOTH] = jnp.zeros((SMOOTH, segs, channels), F32)
    powers[SMOOTH + NF :] = jnp.zeros((SMOOTH, segs, channels), F32)
    block = 12

    def square(step, water):
        first = pl.multiple_of(step * (block * segs), segs)
        second = pl.multiple_of(first + NF * segs, segs)
        real = total[pl.ds(first, block * segs), :] + filtered[pl.ds(first, block * segs), :]
        imag = total[pl.ds(second, block * segs), :] + filtered[pl.ds(second, block * segs), :]
        total[pl.ds(first, block * segs), :] = real
        total[pl.ds(second, block * segs), :] = imag
        power = (real * real + imag * imag).reshape(block, segs, channels)
        powers[pl.ds(step * block + SMOOTH, block)] = power
        return water + power.sum(0)

    water = lax.fori_loop(0, NF // block, square, jnp.zeros((segs, channels), F32))
    floor = water * (water_share / NF) + epsilon
    good = mask[...].astype(F32)
    for k in range(parts):
        start = (me[0] ^ k) * share
        out, base = places[k]

        def spread(step, carry, start=start, out=out, base=base):
            bin_at = start + step * block
            cells = powers[pl.ds(bin_at, block + 2 * SMOOTH)]
            two = cells[:-1] + cells[1:]
            four = two[:-2] + two[2:]
            eight = four[:-4] + four[4:]
            nine = eight[:block] + cells[2 * SMOOTH :]
            scaled = good * lax.rsqrt(nine * (1.0 / (2 * SMOOTH + 1)) + floor)
            first = pl.multiple_of(bin_at * segs, segs)
            second = pl.multiple_of(first + NF * segs, segs)
            real = total[pl.ds(first, block * segs), :].reshape(block, segs, channels) * scaled
            imag = total[pl.ds(second, block * segs), :].reshape(block, segs, channels) * scaled
            both = jnp.concatenate([real[:, None], imag[:, None]], axis=1)
            at = pl.multiple_of(base + step * (block * 2 * segs), 2 * segs)
            out[pl.ds(at, block * 2 * segs), :] = both.reshape(block * 2 * segs, channels).astype(BF16)
            return carry

        lax.fori_loop(0, share // block, spread, 0)
        out[base + share * 2 * segs : base + height, :] = good.astype(BF16)


def whitened_parts(parts, me, taps, filtered, left, right, mask):
    segs, channels = mask.shape
    rows = NF // parts * 2 * segs + segs
    return pl.pallas_call(
        functools.partial(whiten_kernel, parts, taps.shape[0]),
        in_specs=[SCALARS] * 2 + [WHOLE] * 4,
        out_specs=[WHOLE] * 3,
        out_shape=[jax.ShapeDtypeStruct((height, channels), BF16) for height in (rows, rows, 2 * rows)],
        scratch_shapes=[
            pltpu.VMEM((2 * NF * segs, channels), F32),
            pltpu.VMEM((NF + 2 * SMOOTH, segs, channels), F32),
        ],
        compiler_params=pltpu.CompilerParams(vmem_limit_bytes=VMEM),
        name="whiten",
    )(me, taps, filtered, left, right, mask)


def gram_kernel(segs, bins, last, *refs):
    own, later = refs[:2]
    if last:
        before, before_count, out, cells, sems = refs[2:]
    else:
        cells, count_out = refs[2:]
    channels = own.shape[1]
    height = own.shape[0] // 2
    share = cells.shape[0]
    row = lax.broadcasted_iota(jnp.int32, (channels, channels), 0)
    column = lax.broadcasted_iota(jnp.int32, (channels, channels), 1)
    ahead = column > row
    skew = (row + column + 1) % channels

    def pieces(side, first, size):
        rows = [side[pl.ds(base + first, size), :] for base in (0, height)]
        return jnp.concatenate(rows, axis=0)

    mine = pieces(own, height - segs, segs)
    theirs = pieces(later, height - segs, segs)
    count = jnp.where(ahead, dot(mine, mine, TN), dot(mine, theirs, TN))
    if last:
        scale = 1.0 / jnp.maximum(count + before_count[...], 1.0)
    else:
        count_out[...] = count

    def group(step, carry):
        for at in range(bins):
            bin_at = step * bins + at
            first = pl.multiple_of(bin_at * (2 * segs), 2 * segs)
            mine = pieces(own, first, 2 * segs)
            theirs = pieces(later, first, 2 * segs)
            split = mine.astype(F32).reshape(mine.shape[0] // (2 * segs), 2, segs, channels)
            turned = jnp.concatenate([-split[:, 1:], split[:, :1]], axis=1)
            turned = turned.reshape(mine.shape).astype(BF16)
            gram = dot(
                jnp.concatenate([mine, turned], axis=1), jnp.concatenate([mine, theirs], axis=1), TN
            )
            for part in range(2):
                rows = gram[part * channels : (part + 1) * channels]
                band = jnp.where(ahead, rows[:, :channels], rows[:, channels:])
                if last:
                    band = (band + before[bin_at, part * channels : (part + 1) * channels, :]) * scale
                    band = jnp.take_along_axis(band, skew, axis=1, mode="promise_in_bounds")
                    cells[bin_at, pl.ds(part, channels, stride=2), :] = band
                else:
                    cells[bin_at, part * channels : (part + 1) * channels, :] = band
        if last:
            at = pl.ds(step * bins, bins)
            pltpu.make_async_copy(cells.at[at], out.at[at], sems.at[step]).start()
        return carry

    lax.fori_loop(0, share // bins, group, 0)
    if last:
        for step in range(share // bins):
            at = pl.ds(step * bins, bins)
            pltpu.make_async_copy(cells.at[at], out.at[at], sems.at[step]).wait()


def stacked(parts, segs, own, later, before=()):
    channels = own.shape[1]
    share = NF // parts
    bins = 4
    last = bool(before)
    sums = jax.ShapeDtypeStruct((share, 2 * channels, LAGS), F32)
    count = jax.ShapeDtypeStruct((channels, channels), F32)
    scratch = [pltpu.VMEM(sums.shape, F32), pltpu.SemaphoreType.DMA((share // bins,))]
    return pl.pallas_call(
        functools.partial(gram_kernel, segs, bins, last),
        in_specs=[WHOLE] * (2 + len(before)),
        out_specs=ANYWHERE if last else [WHOLE] * 2,
        out_shape=sums if last else [sums, count],
        scratch_shapes=scratch if last else [],
        compiler_params=pltpu.CompilerParams(vmem_limit_bytes=VMEM),
        name="gram",
    )(own, later, *before)


def on_device(fibers, parts, raw_strain, fir_taps, good_mask):
    segs, channels, samples = raw_strain.shape
    basis = basis_rows(samples)
    me = lax.axis_index("seg").astype(jnp.int32)
    head, tail = edge_spectra(basis, raw_strain)
    left = lax.ppermute(tail, "fiber", [(i, i + 1) for i in range(fibers - 1)])
    right = lax.ppermute(head, "fiber", [(i + 1, i) for i in range(fibers - 1)])
    filtered = main_spectra(basis, raw_strain, fir_taps)
    near, far, other = whitened_parts(
        parts, me[None], fir_taps, filtered, left, right, good_mask
    )
    rows = near.shape[0]
    swapped = lax.ppermute(other, "seg", [(j, j ^ 1) for j in range(parts)])
    near = jnp.concatenate([near, swapped[:rows]], axis=0)
    far = jnp.concatenate([far, swapped[rows:]], axis=0)

    def following(cells, flip):
        pairs = [
            ((i + 1) * parts + (j ^ flip), i * parts + j)
            for i in range(fibers - 1)
            for j in range(parts)
        ]
        return lax.ppermute(cells, GRID, pairs)

    later_far = following(far, 2)
    own_far = lax.ppermute(far, "seg", [(j, j ^ 2) for j in range(parts)])
    later_near = following(near, 0)
    before = stacked(parts, segs, near, later_near)
    out = stacked(parts, segs, own_far, later_far, before)
    return out.reshape(out.shape[0], channels, 2, LAGS)


def solution(mesh):
    return jax.shard_map(
        functools.partial(on_device, mesh.shape["fiber"], mesh.shape["seg"]),
        mesh=mesh,
        in_specs=(P("seg", "fiber", None), P(), P("seg", "fiber")),
        out_specs=P("seg", "fiber", None, None),
        check_vma=False,
    )
```

```python
import functools
import math

import jax
import jax.numpy as jnp
import numpy as np
from jax import lax
from jax.experimental import pallas as pl
from jax.experimental.pallas import tpu as pltpu
from jax.sharding import PartitionSpec as P

NF = 144
LOW = 16
SMOOTH = 4
LAGS = 128
EDGE = 16
HALF = 15

epsilon = 1e-06
water_share = 0.1

GRID = ("fiber", "seg")
VMEM = 24 * 1024 * 1024
STREAM = 50 * 1024 * 1024
F32 = jnp.float32
BF16 = jnp.bfloat16


def basis_rows(samples):
    times = np.arange(samples, dtype=np.int64)
    bins = np.arange(NF, dtype=np.int64) + LOW
    phase_index = bins[:, None] * times[None, :] % samples
    angles = phase_index.astype(np.float32) * np.float32(2.0 * math.pi / samples)
    rows = np.concatenate([np.cos(angles), -np.sin(angles)], axis=0)
    return jnp.asarray(rows, dtype=BF16)


def filter_band(taps, count, first, shape):
    offset = lax.broadcasted_iota(jnp.int32, shape, 0) - lax.broadcasted_iota(jnp.int32, shape, 1)
    band = jnp.zeros(shape, F32)
    for tap in range(count):
        band = jnp.where(offset == tap - first - HALF, taps[tap], band)
    return band


NT = (((1,), (1,)), ((), ()))
TN = (((0,), (0,)), ((), ()))


def dot(a, b, dims=(((1,), (0,)), ((), ()))):
    return lax.dot_general(a, b, dims, preferred_element_type=F32)


WHOLE = pl.BlockSpec(memory_space=pltpu.VMEM)
SCALARS = pl.BlockSpec(memory_space=pltpu.SMEM)
ANYWHERE = pl.BlockSpec(memory_space=pl.ANY)


def edge_kernel(first, last, basis, head, tail):
    for cells, out in ((last, tail), (first, head)):
        segs, width, samples = cells.shape
        out[...] = dot(basis[...], cells[...].reshape(segs * width, samples), NT).astype(BF16)


def edge_spectra(basis, raw):
    segs, channels, samples = raw.shape
    out = jax.ShapeDtypeStruct((2 * NF, segs * EDGE), BF16)
    return pl.pallas_call(
        edge_kernel,
        in_specs=[WHOLE] * 3,
        out_specs=[WHOLE] * 2,
        out_shape=[out, out],
        compiler_params=pltpu.CompilerParams(vmem_limit_bytes=VMEM),
        cost_estimate=pl.CostEstimate(flops=1, bytes_accessed=1, transcendentals=0),
        name="edge_spectra",
    )(raw[:, :EDGE], raw[:, channels - EDGE :], basis)


def main_kernel(pair, count, raw, basis, taps, filtered, both):
    segs, channels, samples = raw.shape
    band = filter_band(taps, count, 0, (channels, channels))
    high = band.astype(BF16)
    low = (band - high.astype(F32)).astype(BF16)
    both[...] = jnp.concatenate(
        [
            jnp.concatenate([high, low], axis=1),
            jnp.concatenate([high, jnp.zeros_like(high)], axis=1),
        ],
        axis=0,
    )
    for step in range(segs // pair):
        block = raw[step * pair : (step + 1) * pair].reshape(pair * channels, samples)
        spectra = dot(basis[...], block, NT)
        for at in range(pair):
            part = spectra[:, at * channels : (at + 1) * channels]
            top = part.astype(BF16)
            rest = (part - top.astype(F32)).astype(BF16)
            sums = dot(jnp.concatenate([top, rest], axis=1), both[...])
            sums = sums[:, :channels] + sums[:, channels:]
            filtered[pl.ds(step * pair + at, 2 * NF, stride=segs), :] = sums


def main_spectra(basis, raw, taps):
    segs, channels, samples = raw.shape
    return pl.pallas_call(
        functools.partial(main_kernel, 4, taps.shape[0]),
        in_specs=[WHOLE, WHOLE, SCALARS],
        out_specs=WHOLE,
        out_shape=jax.ShapeDtypeStruct((2 * NF * segs, channels), F32),
        scratch_shapes=[pltpu.VMEM((2 * channels, 2 * channels), BF16)],
        compiler_params=pltpu.CompilerParams(vmem_limit_bytes=VMEM),
        name="main_spectra",
    )(raw, basis, taps)


def whiten_kernel(parts, count, me, taps, filtered, left, right, mask, *refs):
    near, far, other, total, powers = refs
    segs, channels = powers.shape[1:]
    height = near.shape[0]
    places = [(near, 0), (other, 0), (far, 0), (other, height)]
    share = NF // parts
    width = segs * EDGE
    owner = lax.broadcasted_iota(jnp.int32, (2 * width, channels), 0) // EDGE % segs
    wide = jnp.concatenate(
        [filter_band(taps, count, -EDGE, (EDGE, channels))] * segs
        + [filter_band(taps, count, channels, (EDGE, channels))] * segs,
        axis=0,
    )
    sides = jnp.concatenate([left[...], right[...]], axis=1)
    for seg in range(segs):
        at = pl.ds(seg, 2 * NF, stride=segs)
        total[at, :] = dot(sides, jnp.where(owner == seg, wide, 0.0).astype(BF16))
    powers[0:SMOOTH] = jnp.zeros((SMOOTH, segs, channels), F32)
    powers[SMOOTH + NF :] = jnp.zeros((SMOOTH, segs, channels), F32)
    block = 12

    def square(step, water):
        first = pl.multiple_of(step * (block * segs), segs)
        second = pl.multiple_of(first + NF * segs, segs)
        real = total[pl.ds(first, block * segs), :] + filtered[pl.ds(first, block * segs), :]
        imag = total[pl.ds(second, block * segs), :] + filtered[pl.ds(second, block * segs), :]
        total[pl.ds(first, block * segs), :] = real
        total[pl.ds(second, block * segs), :] = imag
        power = (real * real + imag * imag).reshape(block, segs, channels)
        powers[pl.ds(step * block + SMOOTH, block)] = power
        return water + power.sum(0)

    water = lax.fori_loop(0, NF // block, square, jnp.zeros((segs, channels), F32))
    floor = water * (water_share / NF) + epsilon
    good = mask[...].astype(F32)
    for k in range(parts):
        start = (me[0] ^ k) * share
        out, base = places[k]

        def spread(step, carry, start=start, out=out, base=base):
            bin_at = start + step * block
            cells = powers[pl.ds(bin_at, block + 2 * SMOOTH)]
            two = cells[:-1] + cells[1:]
            four = two[:-2] + two[2:]
            eight = four[:-4] + four[4:]
            nine = eight[:block] + cells[2 * SMOOTH :]
            scaled = good * lax.rsqrt(nine * (1.0 / (2 * SMOOTH + 1)) + floor)
            first = pl.multiple_of(bin_at * segs, segs)
            second = pl.multiple_of(first + NF * segs, segs)
            real = total[pl.ds(first, block * segs), :].reshape(block, segs, channels) * scaled
            imag = total[pl.ds(second, block * segs), :].reshape(block, segs, channels) * scaled
            both = jnp.concatenate([real[:, None], imag[:, None]], axis=1)
            at = pl.multiple_of(base + step * (block * 2 * segs), 2 * segs)
            out[pl.ds(at, block * 2 * segs), :] = both.reshape(block * 2 * segs, channels).astype(BF16)
            return carry

        lax.fori_loop(0, share // block, spread, 0)
        out[base + share * 2 * segs : base + height, :] = good.astype(BF16)


def whitened_parts(parts, me, taps, filtered, left, right, mask):
    segs, channels = mask.shape
    rows = NF // parts * 2 * segs + segs
    return pl.pallas_call(
        functools.partial(whiten_kernel, parts, taps.shape[0]),
        in_specs=[SCALARS] * 2 + [WHOLE] * 4,
        out_specs=[WHOLE] * 3,
        out_shape=[jax.ShapeDtypeStruct((height, channels), BF16) for height in (rows, rows, 2 * rows)],
        scratch_shapes=[
            pltpu.VMEM((2 * NF * segs, channels), F32),
            pltpu.VMEM((NF + 2 * SMOOTH, segs, channels), F32),
        ],
        compiler_params=pltpu.CompilerParams(vmem_limit_bytes=VMEM),
        name="whiten",
    )(me, taps, filtered, left, right, mask)


def pieces(arrays, first, size):
    height = arrays[0].shape[0] // 2
    rows = [ref[pl.ds(base + first, size), :] for ref in arrays for base in (0, height)]
    return jnp.concatenate(rows, axis=0)


def own_kernel(segs, bins, near, far, rows, sums, count):
    own = (near, far)
    channels = near.shape[1]
    height = near.shape[0] // 2
    share = rows.shape[0]
    flags = pieces(own, height - segs, segs)
    count[...] = dot(flags, flags, TN)

    def group(step, carry):
        for at in range(bins):
            bin_at = step * bins + at
            first = pl.multiple_of(bin_at * (2 * segs), 2 * segs)
            mine = pieces(own, first, 2 * segs)
            split = mine.reshape(mine.shape[0] // (2 * segs), 2, segs, channels)
            turned = jnp.concatenate([-split[:, 1:], split[:, :1]], axis=1).reshape(mine.shape)
            both = jnp.concatenate([mine.T, turned.T], axis=0)
            rows[bin_at] = both
            sums[bin_at] = dot(both, mine)
        return carry

    lax.fori_loop(0, share // bins, group, 0)


def own_gram(parts, segs, near, far):
    channels = near.shape[1]
    share = NF // parts
    return pl.pallas_call(
        functools.partial(own_kernel, segs, 12),
        in_specs=[WHOLE] * 2,
        out_specs=[WHOLE] * 3,
        out_shape=[
            jax.ShapeDtypeStruct((share, 2 * channels, 2 * parts * segs), BF16),
            jax.ShapeDtypeStruct((share, 2 * channels, channels), F32),
            jax.ShapeDtypeStruct((channels, channels), F32),
        ],
        compiler_params=pltpu.CompilerParams(vmem_limit_bytes=VMEM),
        name="own_gram",
    )(near, far)


def gram_kernel(segs, bins, batch, later_far, later_near, near, far, rows, sums, own_count, out, cells, sems):
    later = (later_near, later_far)
    channels = near.shape[1]
    height = near.shape[0] // 2
    share = rows.shape[0]
    row = lax.broadcasted_iota(jnp.int32, (channels, channels), 0)
    column = lax.broadcasted_iota(jnp.int32, (channels, channels), 1)
    ahead = column > row
    skew = (row + column + 1) % channels
    mine = pieces((near, far), height - segs, segs)
    theirs = pieces(later, height - segs, segs)
    count = jnp.where(ahead, own_count[...], dot(mine, theirs, TN))
    scale = 1.0 / jnp.maximum(count, 1.0)

    def group(step, carry):
        for at in range(bins):
            bin_at = step * bins + at
            first = pl.multiple_of(bin_at * (2 * segs), 2 * segs)
            gram = dot(rows[bin_at], pieces(later, first, 2 * segs))
            for part in range(2):
                half = slice(part * channels, (part + 1) * channels)
                band = jnp.where(ahead, sums[bin_at, half, :], gram[half]) * scale
                band = jnp.take_along_axis(band, skew, axis=1, mode="promise_in_bounds")
                cells[bin_at, pl.ds(part, channels, stride=2), :] = band
            if at % batch == batch - 1:
                done = step * (bins // batch) + at // batch
                there = pl.ds(done * batch, batch)
                pltpu.make_async_copy(cells.at[there], out.at[there], sems.at[done]).start()
        return carry

    lax.fori_loop(0, share // bins, group, 0)
    for done in range(share // batch):
        there = pl.ds(done * batch, batch)
        pltpu.make_async_copy(cells.at[there], out.at[there], sems.at[done]).wait()


def stacked(parts, segs, near, later_near, far, later_far):
    channels = near.shape[1]
    share = NF // parts
    batch = 4
    shape = (share, 2 * channels, LAGS)
    rows, sums, count = own_gram(parts, segs, near, far)
    return pl.pallas_call(
        functools.partial(gram_kernel, segs, 12, batch),
        in_specs=[WHOLE] * 7,
        out_specs=ANYWHERE,
        out_shape=jax.ShapeDtypeStruct(shape, F32),
        scratch_shapes=[pltpu.VMEM(shape, F32), pltpu.SemaphoreType.DMA((share // batch,))],
        compiler_params=pltpu.CompilerParams(vmem_limit_bytes=VMEM),
        name="gram",
    )(later_far, later_near, near, far, rows, sums, count)


def on_device(fibers, parts, raw_strain, fir_taps, good_mask):
    segs, channels, samples = raw_strain.shape
    basis = basis_rows(samples)
    me = lax.axis_index("seg").astype(jnp.int32)
    head, tail = edge_spectra(basis, raw_strain)
    left = lax.ppermute(tail, "fiber", [(i, i + 1) for i in range(fibers - 1)])
    right = lax.ppermute(head, "fiber", [(i + 1, i) for i in range(fibers - 1)])
    filtered = main_spectra(basis, raw_strain, fir_taps)
    near, far, other = whitened_parts(
        parts, me[None], fir_taps, filtered, left, right, good_mask
    )
    rows = near.shape[0]
    swapped = lax.ppermute(other, "seg", [(j, j ^ 1) for j in range(parts)])
    near = jnp.concatenate([near, swapped[:rows]], axis=0)
    far = jnp.concatenate([far, swapped[rows:]], axis=0)

    def following(cells, flip):
        pairs = [
            ((i + 1) * parts + (j ^ flip), i * parts + j)
            for i in range(fibers - 1)
            for j in range(parts)
        ]
        return lax.ppermute(cells, GRID, pairs)

    later_far = following(far, 2)
    own_far = lax.ppermute(far, "seg", [(j, j ^ 2) for j in range(parts)])
    later_near = following(near, 0)
    out = stacked(parts, segs, near, later_near, own_far, later_far)
    return out.reshape(out.shape[0], channels, 2, LAGS)


def solution(mesh):
    return jax.shard_map(
        functools.partial(on_device, mesh.shape["fiber"], mesh.shape["seg"]),
        mesh=mesh,
        in_specs=(P("seg", "fiber", None), P(), P("seg", "fiber")),
        out_specs=P("seg", "fiber", None, None),
        check_vma=False,
    )
```

```python
import functools
import math

import jax
import jax.numpy as jnp
import numpy as np
from jax import lax
from jax.experimental import pallas as pl
from jax.experimental.pallas import tpu as pltpu
from jax.sharding import PartitionSpec as P

NF = 144
LOW = 16
SMOOTH = 4
LAGS = 128
EDGE = 16
HALF = 15

epsilon = 1e-06
water_share = 0.1

GRID = ("fiber", "seg")
AHEAD = 16
VMEM = 24 * 1024 * 1024
STREAM = 50 * 1024 * 1024
F32 = jnp.float32
BF16 = jnp.bfloat16


def basis_rows(samples):
    times = np.arange(samples, dtype=np.int64)
    bins = np.arange(NF, dtype=np.int64) + LOW
    phase_index = bins[:, None] * times[None, :] % samples
    angles = phase_index.astype(np.float32) * np.float32(2.0 * math.pi / samples)
    rows = np.concatenate([np.cos(angles), -np.sin(angles)], axis=0)
    return jnp.asarray(rows, dtype=BF16)


def filter_band(taps, count, first, shape):
    offset = lax.broadcasted_iota(jnp.int32, shape, 0) - lax.broadcasted_iota(jnp.int32, shape, 1)
    band = jnp.zeros(shape, F32)
    for tap in range(count):
        band = jnp.where(offset == tap - first - HALF, taps[tap], band)
    return band


NT = (((1,), (1,)), ((), ()))
TN = (((0,), (0,)), ((), ()))


def dot(a, b, dims=(((1,), (0,)), ((), ()))):
    return lax.dot_general(a, b, dims, preferred_element_type=F32)


WHOLE = pl.BlockSpec(memory_space=pltpu.VMEM)
SCALARS = pl.BlockSpec(memory_space=pltpu.SMEM)
ANYWHERE = pl.BlockSpec(memory_space=pl.ANY)


def edge_kernel(first, last, basis, head, tail):
    for cells, out in ((last, tail), (first, head)):
        segs, width, samples = cells.shape
        out[...] = dot(basis[...], cells[...].reshape(segs * width, samples), NT).astype(BF16)


def edge_spectra(basis, raw):
    segs, channels, samples = raw.shape
    out = jax.ShapeDtypeStruct((2 * NF, segs * EDGE), BF16)
    return pl.pallas_call(
        edge_kernel,
        in_specs=[WHOLE] * 3,
        out_specs=[WHOLE] * 2,
        out_shape=[out, out],
        compiler_params=pltpu.CompilerParams(vmem_limit_bytes=VMEM),
        cost_estimate=pl.CostEstimate(flops=1, bytes_accessed=1, transcendentals=0),
        name="edge_spectra",
    )(raw[:, :EDGE], raw[:, channels - EDGE :], basis)


def main_kernel(pair, count, raw, basis, taps, filtered, both):
    segs, channels, samples = raw.shape
    band = filter_band(taps, count, 0, (channels, channels))
    high = band.astype(BF16)
    low = (band - high.astype(F32)).astype(BF16)
    both[...] = jnp.concatenate(
        [
            jnp.concatenate([high, low], axis=1),
            jnp.concatenate([high, jnp.zeros_like(high)], axis=1),
        ],
        axis=0,
    )
    for step in range(segs // pair):
        block = raw[step * pair : (step + 1) * pair].reshape(pair * channels, samples)
        spectra = dot(basis[...], block, NT)
        for at in range(pair):
            part = spectra[:, at * channels : (at + 1) * channels]
            top = part.astype(BF16)
            rest = (part - top.astype(F32)).astype(BF16)
            sums = dot(jnp.concatenate([top, rest], axis=1), both[...])
            sums = sums[:, :channels] + sums[:, channels:]
            filtered[pl.ds(step * pair + at, 2 * NF, stride=segs), :] = sums


def main_spectra(basis, raw, taps):
    segs, channels, samples = raw.shape
    return pl.pallas_call(
        functools.partial(main_kernel, 4, taps.shape[0]),
        in_specs=[WHOLE, WHOLE, SCALARS],
        out_specs=WHOLE,
        out_shape=jax.ShapeDtypeStruct((2 * NF * segs, channels), F32),
        scratch_shapes=[pltpu.VMEM((2 * channels, 2 * channels), BF16)],
        compiler_params=pltpu.CompilerParams(vmem_limit_bytes=VMEM),
        name="main_spectra",
    )(raw, basis, taps)


def whiten_kernel(parts, count, me, taps, filtered, left, right, mask, *refs):
    near, far, other, total, powers = refs
    segs, channels = powers.shape[1:]
    height = near.shape[0]
    places = [(near, 0), (other, 0), (far, 0), (other, height)]
    share = NF // parts
    width = segs * EDGE
    owner = lax.broadcasted_iota(jnp.int32, (2 * width, channels), 0) // EDGE % segs
    wide = jnp.concatenate(
        [filter_band(taps, count, -EDGE, (EDGE, channels))] * segs
        + [filter_band(taps, count, channels, (EDGE, channels))] * segs,
        axis=0,
    )
    sides = jnp.concatenate([left[...], right[...]], axis=1)
    for seg in range(segs):
        at = pl.ds(seg, 2 * NF, stride=segs)
        total[at, :] = dot(sides, jnp.where(owner == seg, wide, 0.0).astype(BF16))
    powers[0:SMOOTH] = jnp.zeros((SMOOTH, segs, channels), F32)
    powers[SMOOTH + NF :] = jnp.zeros((SMOOTH, segs, channels), F32)
    block = 12

    def square(step, water):
        first = pl.multiple_of(step * (block * segs), segs)
        second = pl.multiple_of(first + NF * segs, segs)
        real = total[pl.ds(first, block * segs), :] + filtered[pl.ds(first, block * segs), :]
        imag = total[pl.ds(second, block * segs), :] + filtered[pl.ds(second, block * segs), :]
        total[pl.ds(first, block * segs), :] = real
        total[pl.ds(second, block * segs), :] = imag
        power = (real * real + imag * imag).reshape(block, segs, channels)
        powers[pl.ds(step * block + SMOOTH, block)] = power
        return water + power.sum(0)

    water = lax.fori_loop(0, NF // block, square, jnp.zeros((segs, channels), F32))
    floor = water * (water_share / NF) + epsilon
    good = mask[...].astype(F32)
    for k in range(parts):
        start = (me[0] ^ k) * share
        out, base = places[k]

        def spread(step, carry, start=start, out=out, base=base):
            bin_at = start + step * block
            cells = powers[pl.ds(bin_at, block + 2 * SMOOTH)]
            two = cells[:-1] + cells[1:]
            four = two[:-2] + two[2:]
            eight = four[:-4] + four[4:]
            nine = eight[:block] + cells[2 * SMOOTH :]
            scaled = good * lax.rsqrt(nine * (1.0 / (2 * SMOOTH + 1)) + floor)
            first = pl.multiple_of(bin_at * segs, segs)
            second = pl.multiple_of(first + NF * segs, segs)
            real = total[pl.ds(first, block * segs), :].reshape(block, segs, channels) * scaled
            imag = total[pl.ds(second, block * segs), :].reshape(block, segs, channels) * scaled
            both = jnp.concatenate([real[:, None], imag[:, None]], axis=1)
            at = pl.multiple_of(base + step * (block * 2 * segs), 2 * segs)
            out[pl.ds(at, block * 2 * segs), :] = both.reshape(block * 2 * segs, channels).astype(BF16)
            return carry

        lax.fori_loop(0, share // block, spread, 0)
        out[base + share * 2 * segs : base + height, :] = good.astype(BF16)


def whitened_parts(parts, me, taps, filtered, left, right, mask):
    segs, channels = mask.shape
    rows = NF // parts * 2 * segs + segs
    return pl.pallas_call(
        functools.partial(whiten_kernel, parts, taps.shape[0]),
        in_specs=[SCALARS] * 2 + [WHOLE] * 4,
        out_specs=[WHOLE] * 3,
        out_shape=[jax.ShapeDtypeStruct((height, channels), BF16) for height in (rows, rows, 2 * rows)],
        scratch_shapes=[
            pltpu.VMEM((2 * NF * segs, channels), F32),
            pltpu.VMEM((NF + 2 * SMOOTH, segs, channels), F32),
        ],
        compiler_params=pltpu.CompilerParams(vmem_limit_bytes=VMEM),
        name="whiten",
    )(me, taps, filtered, left, right, mask)


def pieces(arrays, first, size):
    height = arrays[0].shape[0] // 2
    rows = [ref[pl.ds(base + first, size), :] for ref in arrays for base in (0, height)]
    return jnp.concatenate(rows, axis=0)


def own_kernel(segs, bins, near, far, rows, sums, count):
    own = (near, far)
    channels = near.shape[1]
    height = near.shape[0] // 2
    share = rows.shape[0]
    flags = pieces(own, height - segs, segs)
    count[...] = dot(flags, flags, TN)

    def group(step, carry):
        for at in range(bins):
            bin_at = step * bins + at
            first = pl.multiple_of(bin_at * (2 * segs), 2 * segs)
            mine = pieces(own, first, 2 * segs)
            split = mine.reshape(mine.shape[0] // (2 * segs), 2, segs, channels)
            turned = jnp.concatenate([-split[:, 1:], split[:, :1]], axis=1).reshape(mine.shape)
            both = jnp.concatenate([mine.T, turned.T], axis=0)
            rows[bin_at] = both
            sums[bin_at] = dot(both, mine)
        return carry

    lax.fori_loop(0, share // bins, group, 0)


def own_gram(parts, segs, near, far):
    channels = near.shape[1]
    share = NF // parts
    return pl.pallas_call(
        functools.partial(own_kernel, segs, 12),
        in_specs=[WHOLE] * 2,
        out_specs=[WHOLE] * 3,
        out_shape=[
            jax.ShapeDtypeStruct((share, 2 * channels, 2 * parts * segs), BF16),
            jax.ShapeDtypeStruct((share, 2 * channels, channels), F32),
            jax.ShapeDtypeStruct((channels, channels), F32),
        ],
        compiler_params=pltpu.CompilerParams(vmem_limit_bytes=VMEM),
        name="own_gram",
    )(near, far)


def gram_kernel(segs, batch, first_half, *refs):
    if first_half:
        later_near, later_far, near, far, own_count, rows, sums, out, scale, cells, sems = refs
        begin = 0
    else:
        later_near, later_far, scale, rows, sums, _, out, cells, sems = refs
        begin = out.shape[0] - cells.shape[0]
    channels = later_near.shape[1]
    count = cells.shape[0]
    bins = count
    row = lax.broadcasted_iota(jnp.int32, (channels, channels), 0)
    column = lax.broadcasted_iota(jnp.int32, (channels, channels), 1)
    ahead = column > row
    skew = (row + column + 1) % channels
    near_height = count * 2 * segs
    far_height = later_far.shape[0] // 2

    def group_rows(ref, height, first, size):
        return [ref[pl.ds(base + first, size), :] for base in (0, height)]

    if first_half:
        height = near.shape[0] // 2
        mine = pieces((near, far), height - segs, segs)
        theirs = jnp.concatenate(
            [later_near[2 * near_height :, :]]
            + group_rows(later_far, far_height, far_height - segs, segs),
            axis=0,
        )
        pairs = jnp.where(ahead, own_count[...], dot(mine, theirs, TN))
        scale[...] = 1.0 / jnp.maximum(pairs, 1.0)

    def group(step, carry):
        for at in range(bins):
            here = step * bins + at
            first = pl.multiple_of(here * (2 * segs), 2 * segs)
            theirs = jnp.concatenate(
                group_rows(later_near, near_height, first, 2 * segs)
                + group_rows(later_far, far_height, first + begin * 2 * segs, 2 * segs),
                axis=0,
            )
            gram = dot(rows[begin + here], theirs)
            for part in range(2):
                half = slice(part * channels, (part + 1) * channels)
                band = jnp.where(ahead, sums[begin + here, half, :], gram[half]) * scale[...]
                band = jnp.take_along_axis(band, skew, axis=1, mode="promise_in_bounds")
                cells[here, pl.ds(part, channels, stride=2), :] = band
            if at % batch == batch - 1:
                done = step * (bins // batch) + at // batch
                pltpu.make_async_copy(
                    cells.at[pl.ds(done * batch, batch)],
                    out.at[pl.ds(begin + done * batch, batch)],
                    sems.at[done],
                ).start()
        return carry

    lax.fori_loop(0, count // bins, group, 0)
    for done in range(count // batch):
        pltpu.make_async_copy(
            cells.at[pl.ds(done * batch, batch)],
            out.at[pl.ds(begin + done * batch, batch)],
            sems.at[done],
        ).wait()


def stacked(parts, segs, near, later_near, far, later_far):
    channels = near.shape[1]
    share = NF // parts
    batch = 4
    rows, sums, count = own_gram(parts, segs, near, far)
    out = jax.ShapeDtypeStruct((share, 2 * channels, LAGS), F32)
    options = lambda bins: dict(
        scratch_shapes=[
            pltpu.VMEM((bins, 2 * channels, LAGS), F32),
            pltpu.SemaphoreType.DMA((bins // batch,)),
        ],
        compiler_params=pltpu.CompilerParams(vmem_limit_bytes=VMEM),
    )
    out, scale = pl.pallas_call(
        functools.partial(gram_kernel, segs, batch, True),
        in_specs=[WHOLE] * 7,
        out_specs=[ANYWHERE, WHOLE],
        out_shape=[out, jax.ShapeDtypeStruct((channels, channels), F32)],
        name="gram",
        **options(AHEAD),
    )(later_near[0], later_far, near, far, count, rows, sums)
    return pl.pallas_call(
        functools.partial(gram_kernel, segs, batch, False),
        in_specs=[WHOLE] * 5 + [ANYWHERE],
        out_specs=ANYWHERE,
        out_shape=jax.ShapeDtypeStruct(out.shape, F32),
        input_output_aliases={5: 0},
        name="gram_last",
        **options(share - AHEAD),
    )(later_near[1], later_far, scale, rows, sums, out)


def on_device(fibers, parts, raw_strain, fir_taps, good_mask):
    segs, channels, samples = raw_strain.shape
    basis = basis_rows(samples)
    me = lax.axis_index("seg").astype(jnp.int32)
    head, tail = edge_spectra(basis, raw_strain)
    left = lax.ppermute(tail, "fiber", [(i, i + 1) for i in range(fibers - 1)])
    right = lax.ppermute(head, "fiber", [(i + 1, i) for i in range(fibers - 1)])
    filtered = main_spectra(basis, raw_strain, fir_taps)
    near, far, other = whitened_parts(
        parts, me[None], fir_taps, filtered, left, right, good_mask
    )
    rows = near.shape[0]
    swapped = lax.ppermute(other, "seg", [(j, j ^ 1) for j in range(parts)])
    near = jnp.concatenate([near, swapped[:rows]], axis=0)
    far = jnp.concatenate([far, swapped[rows:]], axis=0)

    def following(cells, flip):
        pairs = [
            ((i + 1) * parts + (j ^ flip), i * parts + j)
            for i in range(fibers - 1)
            for j in range(parts)
        ]
        return lax.ppermute(cells, GRID, pairs)

    later_far = following(far, 2)
    own_far = lax.ppermute(far, "seg", [(j, j ^ 2) for j in range(parts)])
    middle = AHEAD * 2 * segs
    cut = lambda begin, stop: [near[begin:stop], near[rows + begin : rows + stop]]
    flags = cut(rows - segs, rows)
    later_near = [
        following(jnp.concatenate(cells, axis=0), 0)
        for cells in (cut(0, middle) + flags, cut(middle, rows - segs))
    ]
    out = stacked(parts, segs, near, later_near, own_far, later_far)
    return out.reshape(out.shape[0], channels, 2, LAGS)


def solution(mesh):
    return jax.shard_map(
        functools.partial(on_device, mesh.shape["fiber"], mesh.shape["seg"]),
        mesh=mesh,
        in_specs=(P("seg", "fiber", None), P(), P("seg", "fiber")),
        out_specs=P("seg", "fiber", None, None),
        check_vma=False,
    )
```

```python
import functools
import math

import jax
import jax.numpy as jnp
import numpy as np
from jax import lax
from jax.experimental import pallas as pl
from jax.experimental.pallas import tpu as pltpu
from jax.sharding import PartitionSpec as P

NF = 144
LOW = 16
SMOOTH = 4
LAGS = 128
EDGE = 16
HALF = 15

epsilon = 1e-06
water_share = 0.1

GRID = ("fiber", "seg")
AHEAD = 16
VMEM = 24 * 1024 * 1024
STREAM = 50 * 1024 * 1024
F32 = jnp.float32
BF16 = jnp.bfloat16


def basis_rows(samples):
    times = np.arange(samples, dtype=np.int64)
    bins = np.arange(NF, dtype=np.int64) + LOW
    phase_index = bins[:, None] * times[None, :] % samples
    angles = phase_index.astype(np.float32) * np.float32(2.0 * math.pi / samples)
    rows = np.concatenate([np.cos(angles), -np.sin(angles)], axis=0)
    return jnp.asarray(rows, dtype=BF16)


def filter_band(taps, count, first, shape):
    offset = lax.broadcasted_iota(jnp.int32, shape, 0) - lax.broadcasted_iota(jnp.int32, shape, 1)
    band = jnp.zeros(shape, F32)
    for tap in range(count):
        band = jnp.where(offset == tap - first - HALF, taps[tap], band)
    return band


NT = (((1,), (1,)), ((), ()))
TN = (((0,), (0,)), ((), ()))


def dot(a, b, dims=(((1,), (0,)), ((), ()))):
    return lax.dot_general(a, b, dims, preferred_element_type=F32)


WHOLE = pl.BlockSpec(memory_space=pltpu.VMEM)
SCALARS = pl.BlockSpec(memory_space=pltpu.SMEM)
ANYWHERE = pl.BlockSpec(memory_space=pl.ANY)


def edge_kernel(first, last, basis, head, tail):
    for cells, out in ((last, tail), (first, head)):
        segs, width, samples = cells.shape
        out[...] = dot(basis[...], cells[...].reshape(segs * width, samples), NT).astype(BF16)


def edge_spectra(basis, raw):
    segs, channels, samples = raw.shape
    out = jax.ShapeDtypeStruct((2 * NF, segs * EDGE), BF16)
    return pl.pallas_call(
        edge_kernel,
        in_specs=[WHOLE] * 3,
        out_specs=[WHOLE] * 2,
        out_shape=[out, out],
        compiler_params=pltpu.CompilerParams(vmem_limit_bytes=VMEM),
        cost_estimate=pl.CostEstimate(flops=1, bytes_accessed=1, transcendentals=0),
        name="edge_spectra",
    )(raw[:, :EDGE], raw[:, channels - EDGE :], basis)


def main_kernel(pair, count, raw, basis, taps, filtered, both):
    segs, channels, samples = raw.shape
    band = filter_band(taps, count, 0, (channels, channels))
    high = band.astype(BF16)
    low = (band - high.astype(F32)).astype(BF16)
    both[...] = jnp.concatenate(
        [
            jnp.concatenate([high, low], axis=1),
            jnp.concatenate([high, jnp.zeros_like(high)], axis=1),
        ],
        axis=0,
    )
    for step in range(segs // pair):
        block = raw[step * pair : (step + 1) * pair].reshape(pair * channels, samples)
        spectra = dot(basis[...], block, NT)
        for at in range(pair):
            part = spectra[:, at * channels : (at + 1) * channels]
            top = part.astype(BF16)
            rest = (part - top.astype(F32)).astype(BF16)
            sums = dot(jnp.concatenate([top, rest], axis=1), both[...])
            sums = sums[:, :channels] + sums[:, channels:]
            filtered[pl.ds(step * pair + at, 2 * NF, stride=segs), :] = sums


def main_spectra(basis, raw, taps):
    segs, channels, samples = raw.shape
    return pl.pallas_call(
        functools.partial(main_kernel, 4, taps.shape[0]),
        in_specs=[WHOLE, WHOLE, SCALARS],
        out_specs=WHOLE,
        out_shape=jax.ShapeDtypeStruct((2 * NF * segs, channels), F32),
        scratch_shapes=[pltpu.VMEM((2 * channels, 2 * channels), BF16)],
        compiler_params=pltpu.CompilerParams(vmem_limit_bytes=VMEM),
        name="main_spectra",
    )(raw, basis, taps)


def whiten_kernel(parts, count, me, taps, filtered, left, right, mask, *refs):
    near, far, other, total, powers = refs
    segs, channels = powers.shape[1:]
    height = near.shape[0]
    places = [(near, 0), (other, 0), (far, 0), (other, height)]
    share = NF // parts
    width = segs * EDGE
    owner = lax.broadcasted_iota(jnp.int32, (2 * width, channels), 0) // EDGE % segs
    wide = jnp.concatenate(
        [filter_band(taps, count, -EDGE, (EDGE, channels))] * segs
        + [filter_band(taps, count, channels, (EDGE, channels))] * segs,
        axis=0,
    )
    sides = jnp.concatenate([left[...], right[...]], axis=1)
    for seg in range(segs):
        at = pl.ds(seg, 2 * NF, stride=segs)
        total[at, :] = dot(sides, jnp.where(owner == seg, wide, 0.0).astype(BF16))
    powers[0:SMOOTH] = jnp.zeros((SMOOTH, segs, channels), F32)
    powers[SMOOTH + NF :] = jnp.zeros((SMOOTH, segs, channels), F32)
    block = 12

    def square(step, water):
        first = pl.multiple_of(step * (block * segs), segs)
        second = pl.multiple_of(first + NF * segs, segs)
        real = total[pl.ds(first, block * segs), :] + filtered[pl.ds(first, block * segs), :]
        imag = total[pl.ds(second, block * segs), :] + filtered[pl.ds(second, block * segs), :]
        total[pl.ds(first, block * segs), :] = real
        total[pl.ds(second, block * segs), :] = imag
        power = (real * real + imag * imag).reshape(block, segs, channels)
        powers[pl.ds(step * block + SMOOTH, block)] = power
        return water + power.sum(0)

    water = lax.fori_loop(0, NF // block, square, jnp.zeros((segs, channels), F32))
    floor = water * (water_share / NF) + epsilon
    good = mask[...].astype(F32)
    for k in range(parts):
        start = (me[0] ^ k) * share
        out, base = places[k]

        def spread(step, carry, start=start, out=out, base=base):
            bin_at = start + step * block
            cells = powers[pl.ds(bin_at, block + 2 * SMOOTH)]
            two = cells[:-1] + cells[1:]
            four = two[:-2] + two[2:]
            eight = four[:-4] + four[4:]
            nine = eight[:block] + cells[2 * SMOOTH :]
            scaled = good * lax.rsqrt(nine * (1.0 / (2 * SMOOTH + 1)) + floor)
            first = pl.multiple_of(bin_at * segs, segs)
            second = pl.multiple_of(first + NF * segs, segs)
            real = total[pl.ds(first, block * segs), :].reshape(block, segs, channels) * scaled
            imag = total[pl.ds(second, block * segs), :].reshape(block, segs, channels) * scaled
            both = jnp.concatenate([real[:, None], imag[:, None]], axis=1)
            at = pl.multiple_of(base + step * (block * 2 * segs), 2 * segs)
            out[pl.ds(at, block * 2 * segs), :] = both.reshape(block * 2 * segs, channels).astype(BF16)
            return carry

        lax.fori_loop(0, share // block, spread, 0)
        out[base + share * 2 * segs : base + height, :] = good.astype(BF16)


def whitened_parts(parts, me, taps, filtered, left, right, mask):
    segs, channels = mask.shape
    rows = NF // parts * 2 * segs + segs
    return pl.pallas_call(
        functools.partial(whiten_kernel, parts, taps.shape[0]),
        in_specs=[SCALARS] * 2 + [WHOLE] * 4,
        out_specs=[WHOLE] * 3,
        out_shape=[jax.ShapeDtypeStruct((height, channels), BF16) for height in (rows, rows, 2 * rows)],
        scratch_shapes=[
            pltpu.VMEM((2 * NF * segs, channels), F32),
            pltpu.VMEM((NF + 2 * SMOOTH, segs, channels), F32),
        ],
        compiler_params=pltpu.CompilerParams(vmem_limit_bytes=VMEM),
        name="whiten",
    )(me, taps, filtered, left, right, mask)


def pieces(arrays, height, first, size):
    rows = [
        ref[pl.ds(base + first, size), :]
        for ref in arrays
        for base in range(0, ref.shape[0], height)
    ]
    return jnp.concatenate(rows, axis=0)


def own_kernel(segs, bins, near, far, far_other, rows, sums, count):
    own = (near, far, far_other)
    height, channels = far.shape
    share = rows.shape[0]
    flags = pieces(own, height, height - segs, segs)
    count[...] = dot(flags, flags, TN)

    def group(step, carry):
        for at in range(bins):
            bin_at = step * bins + at
            first = pl.multiple_of(bin_at * (2 * segs), 2 * segs)
            mine = pieces(own, height, first, 2 * segs)
            split = mine.reshape(mine.shape[0] // (2 * segs), 2, segs, channels)
            turned = jnp.concatenate([-split[:, 1:], split[:, :1]], axis=1).reshape(mine.shape)
            both = jnp.concatenate([mine.T, turned.T], axis=0)
            rows[bin_at] = both
            sums[bin_at] = dot(both, mine)
        return carry

    lax.fori_loop(0, share // bins, group, 0)


def own_gram(parts, segs, near, far, far_other):
    channels = near.shape[1]
    share = NF // parts
    return pl.pallas_call(
        functools.partial(own_kernel, segs, 12),
        in_specs=[WHOLE] * 3,
        out_specs=[WHOLE] * 3,
        out_shape=[
            jax.ShapeDtypeStruct((share, 2 * channels, 2 * parts * segs), BF16),
            jax.ShapeDtypeStruct((share, 2 * channels, channels), F32),
            jax.ShapeDtypeStruct((channels, channels), F32),
        ],
        compiler_params=pltpu.CompilerParams(vmem_limit_bytes=VMEM),
        name="own_gram",
    )(near, far, far_other)


def gram_kernel(segs, batch, first_half, *refs):
    if first_half:
        later_near, later_far, near, far, far_other, own_count, rows, sums, out, scale, cells, sems = refs
        begin = 0
    else:
        later_near, later_far, scale, rows, sums, _, out, cells, sems = refs
        begin = out.shape[0] - cells.shape[0]
    channels = later_near.shape[1]
    count = cells.shape[0]
    bins = count
    row = lax.broadcasted_iota(jnp.int32, (channels, channels), 0)
    column = lax.broadcasted_iota(jnp.int32, (channels, channels), 1)
    ahead = column > row
    skew = (row + column + 1) % channels
    near_height = count * 2 * segs
    far_height = later_far.shape[0] // 2

    def group_rows(ref, height, first, size):
        return [ref[pl.ds(base + first, size), :] for base in (0, height)]

    if first_half:
        height = far.shape[0]
        mine = pieces((near, far, far_other), height, height - segs, segs)
        theirs = jnp.concatenate(
            [later_near[2 * near_height :, :]]
            + group_rows(later_far, far_height, far_height - segs, segs),
            axis=0,
        )
        pairs = jnp.where(ahead, own_count[...], dot(mine, theirs, TN))
        scale[...] = 1.0 / jnp.maximum(pairs, 1.0)

    def group(step, carry):
        for at in range(bins):
            here = step * bins + at
            first = pl.multiple_of(here * (2 * segs), 2 * segs)
            theirs = jnp.concatenate(
                group_rows(later_near, near_height, first, 2 * segs)
                + group_rows(later_far, far_height, first + begin * 2 * segs, 2 * segs),
                axis=0,
            )
            gram = dot(rows[begin + here], theirs)
            for part in range(2):
                half = slice(part * channels, (part + 1) * channels)
                band = jnp.where(ahead, sums[begin + here, half, :], gram[half]) * scale[...]
                band = jnp.take_along_axis(band, skew, axis=1, mode="promise_in_bounds")
                cells[here, pl.ds(part, channels, stride=2), :] = band
            if at % batch == batch - 1:
                done = step * (bins // batch) + at // batch
                pltpu.make_async_copy(
                    cells.at[pl.ds(done * batch, batch)],
                    out.at[pl.ds(begin + done * batch, batch)],
                    sems.at[done],
                ).start()
        return carry

    lax.fori_loop(0, count // bins, group, 0)
    for done in range(count // batch):
        pltpu.make_async_copy(
            cells.at[pl.ds(done * batch, batch)],
            out.at[pl.ds(begin + done * batch, batch)],
            sems.at[done],
        ).wait()


def stacked(parts, segs, near, later_near, far, later_far):
    channels = near.shape[1]
    share = NF // parts
    batch = 4
    rows, sums, count = own_gram(parts, segs, near, *far)
    out = jax.ShapeDtypeStruct((share, 2 * channels, LAGS), F32)
    options = lambda bins: dict(
        scratch_shapes=[
            pltpu.VMEM((bins, 2 * channels, LAGS), F32),
            pltpu.SemaphoreType.DMA((bins // batch,)),
        ],
        compiler_params=pltpu.CompilerParams(vmem_limit_bytes=VMEM),
    )
    out, scale = pl.pallas_call(
        functools.partial(gram_kernel, segs, batch, True),
        in_specs=[WHOLE] * 8,
        out_specs=[ANYWHERE, WHOLE],
        out_shape=[out, jax.ShapeDtypeStruct((channels, channels), F32)],
        name="gram",
        **options(AHEAD),
    )(later_near[0], later_far, near, *far, count, rows, sums)
    return pl.pallas_call(
        functools.partial(gram_kernel, segs, batch, False),
        in_specs=[WHOLE] * 5 + [ANYWHERE],
        out_specs=ANYWHERE,
        out_shape=jax.ShapeDtypeStruct(out.shape, F32),
        input_output_aliases={5: 0},
        name="gram_last",
        **options(share - AHEAD),
    )(later_near[1], later_far, scale, rows, sums, out)


def on_device(fibers, parts, raw_strain, fir_taps, good_mask):
    segs, channels, samples = raw_strain.shape
    basis = basis_rows(samples)
    me = lax.axis_index("seg").astype(jnp.int32)
    head, tail = edge_spectra(basis, raw_strain)
    left = lax.ppermute(tail, "fiber", [(i, i + 1) for i in range(fibers - 1)])
    right = lax.ppermute(head, "fiber", [(i + 1, i) for i in range(fibers - 1)])
    filtered = main_spectra(basis, raw_strain, fir_taps)
    near, far, other = whitened_parts(
        parts, me[None], fir_taps, filtered, left, right, good_mask
    )
    rows = near.shape[0]
    swapped = lax.ppermute(other, "seg", [(j, j ^ 1) for j in range(parts)])
    across = [(j, j ^ 2) for j in range(parts)]
    own_far = [lax.ppermute(cells, "seg", across) for cells in (far, swapped[rows:])]
    near = jnp.concatenate([near, swapped[:rows]], axis=0)
    far = jnp.concatenate([far, swapped[rows:]], axis=0)

    def following(cells, flip):
        pairs = [
            ((i + 1) * parts + (j ^ flip), i * parts + j)
            for i in range(fibers - 1)
            for j in range(parts)
        ]
        return lax.ppermute(cells, GRID, pairs)

    later_far = following(far, 2)
    middle = AHEAD * 2 * segs
    cut = lambda begin, stop: [near[begin:stop], near[rows + begin : rows + stop]]
    flags = cut(rows - segs, rows)
    later_near = [
        following(jnp.concatenate(cells, axis=0), 0)
        for cells in (cut(0, middle) + flags, cut(middle, rows - segs))
    ]
    out = stacked(parts, segs, near, later_near, own_far, later_far)
    return out.reshape(out.shape[0], channels, 2, LAGS)


def solution(mesh):
    return jax.shard_map(
        functools.partial(on_device, mesh.shape["fiber"], mesh.shape["seg"]),
        mesh=mesh,
        in_specs=(P("seg", "fiber", None), P(), P("seg", "fiber")),
        out_specs=P("seg", "fiber", None, None),
        check_vma=False,
    )
```

```python
import functools
import math

import jax
import jax.numpy as jnp
import numpy as np
from jax import lax
from jax.experimental import pallas as pl
from jax.experimental.pallas import tpu as pltpu
from jax.sharding import PartitionSpec as P

NF = 144
LOW = 16
SMOOTH = 4
LAGS = 128
EDGE = 16
HALF = 15

epsilon = 1e-06
water_share = 0.1

GRID = ("fiber", "seg")
CUTS = (0, 10, 22, 36)
VMEM = 24 * 1024 * 1024
STREAM = 50 * 1024 * 1024
F32 = jnp.float32
BF16 = jnp.bfloat16


def basis_rows(samples):
    times = np.arange(samples, dtype=np.int64)
    bins = np.arange(NF, dtype=np.int64) + LOW
    phase_index = bins[:, None] * times[None, :] % samples
    angles = phase_index.astype(np.float32) * np.float32(2.0 * math.pi / samples)
    rows = np.concatenate([np.cos(angles), -np.sin(angles)], axis=0)
    return jnp.asarray(rows, dtype=BF16)


def filter_band(taps, count, first, shape):
    offset = lax.broadcasted_iota(jnp.int32, shape, 0) - lax.broadcasted_iota(jnp.int32, shape, 1)
    band = jnp.zeros(shape, F32)
    for tap in range(count):
        band = jnp.where(offset == tap - first - HALF, taps[tap], band)
    return band


NT = (((1,), (1,)), ((), ()))
TN = (((0,), (0,)), ((), ()))


def dot(a, b, dims=(((1,), (0,)), ((), ()))):
    return lax.dot_general(a, b, dims, preferred_element_type=F32)


WHOLE = pl.BlockSpec(memory_space=pltpu.VMEM)
SCALARS = pl.BlockSpec(memory_space=pltpu.SMEM)
ANYWHERE = pl.BlockSpec(memory_space=pl.ANY)


def edge_kernel(first, last, basis, head, tail):
    for cells, out in ((last, tail), (first, head)):
        segs, width, samples = cells.shape
        out[...] = dot(basis[...], cells[...].reshape(segs * width, samples), NT).astype(BF16)


def edge_spectra(basis, raw):
    segs, channels, samples = raw.shape
    out = jax.ShapeDtypeStruct((2 * NF, segs * EDGE), BF16)
    return pl.pallas_call(
        edge_kernel,
        in_specs=[WHOLE] * 3,
        out_specs=[WHOLE] * 2,
        out_shape=[out, out],
        compiler_params=pltpu.CompilerParams(vmem_limit_bytes=VMEM),
        cost_estimate=pl.CostEstimate(flops=1, bytes_accessed=1, transcendentals=0),
        name="edge_spectra",
    )(raw[:, :EDGE], raw[:, channels - EDGE :], basis)


def main_kernel(pair, count, raw, basis, taps, filtered, both):
    segs, channels, samples = raw.shape
    band = filter_band(taps, count, 0, (channels, channels))
    high = band.astype(BF16)
    low = (band - high.astype(F32)).astype(BF16)
    both[...] = jnp.concatenate(
        [
            jnp.concatenate([high, low], axis=1),
            jnp.concatenate([high, jnp.zeros_like(high)], axis=1),
        ],
        axis=0,
    )
    for step in range(segs // pair):
        block = raw[step * pair : (step + 1) * pair].reshape(pair * channels, samples)
        spectra = dot(basis[...], block, NT)
        for at in range(pair):
            part = spectra[:, at * channels : (at + 1) * channels]
            top = part.astype(BF16)
            rest = (part - top.astype(F32)).astype(BF16)
            sums = dot(jnp.concatenate([top, rest], axis=1), both[...])
            sums = sums[:, :channels] + sums[:, channels:]
            filtered[pl.ds(step * pair + at, 2 * NF, stride=segs), :] = sums


def main_spectra(basis, raw, taps):
    segs, channels, samples = raw.shape
    return pl.pallas_call(
        functools.partial(main_kernel, 4, taps.shape[0]),
        in_specs=[WHOLE, WHOLE, SCALARS],
        out_specs=WHOLE,
        out_shape=jax.ShapeDtypeStruct((2 * NF * segs, channels), F32),
        scratch_shapes=[pltpu.VMEM((2 * channels, 2 * channels), BF16)],
        compiler_params=pltpu.CompilerParams(vmem_limit_bytes=VMEM),
        name="main_spectra",
    )(raw, basis, taps)


def whiten_kernel(parts, count, me, taps, filtered, left, right, mask, *refs):
    near, far, other, total, powers = refs
    segs, channels = powers.shape[1:]
    height = near.shape[0]
    places = [(near, 0), (other, 0), (far, 0), (other, height)]
    share = NF // parts
    width = segs * EDGE
    owner = lax.broadcasted_iota(jnp.int32, (2 * width, channels), 0) // EDGE % segs
    wide = jnp.concatenate(
        [filter_band(taps, count, -EDGE, (EDGE, channels))] * segs
        + [filter_band(taps, count, channels, (EDGE, channels))] * segs,
        axis=0,
    )
    sides = jnp.concatenate([left[...], right[...]], axis=1)
    for seg in range(segs):
        at = pl.ds(seg, 2 * NF, stride=segs)
        total[at, :] = dot(sides, jnp.where(owner == seg, wide, 0.0).astype(BF16))
    powers[0:SMOOTH] = jnp.zeros((SMOOTH, segs, channels), F32)
    powers[SMOOTH + NF :] = jnp.zeros((SMOOTH, segs, channels), F32)
    block = 12

    def square(step, water):
        first = pl.multiple_of(step * (block * segs), segs)
        second = pl.multiple_of(first + NF * segs, segs)
        real = total[pl.ds(first, block * segs), :] + filtered[pl.ds(first, block * segs), :]
        imag = total[pl.ds(second, block * segs), :] + filtered[pl.ds(second, block * segs), :]
        total[pl.ds(first, block * segs), :] = real
        total[pl.ds(second, block * segs), :] = imag
        power = (real * real + imag * imag).reshape(block, segs, channels)
        powers[pl.ds(step * block + SMOOTH, block)] = power
        return water + power.sum(0)

    water = lax.fori_loop(0, NF // block, square, jnp.zeros((segs, channels), F32))
    floor = water * (water_share / NF) + epsilon
    good = mask[...].astype(F32)
    for k in range(parts):
        start = (me[0] ^ k) * share
        out, base = places[k]

        def spread(step, carry, start=start, out=out, base=base):
            bin_at = start + step * block
            cells = powers[pl.ds(bin_at, block + 2 * SMOOTH)]
            two = cells[:-1] + cells[1:]
            four = two[:-2] + two[2:]
            eight = four[:-4] + four[4:]
            nine = eight[:block] + cells[2 * SMOOTH :]
            scaled = good * lax.rsqrt(nine * (1.0 / (2 * SMOOTH + 1)) + floor)
            first = pl.multiple_of(bin_at * segs, segs)
            second = pl.multiple_of(first + NF * segs, segs)
            real = total[pl.ds(first, block * segs), :].reshape(block, segs, channels) * scaled
            imag = total[pl.ds(second, block * segs), :].reshape(block, segs, channels) * scaled
            both = jnp.concatenate([real[:, None], imag[:, None]], axis=1)
            at = pl.multiple_of(base + step * (block * 2 * segs), 2 * segs)
            out[pl.ds(at, block * 2 * segs), :] = both.reshape(block * 2 * segs, channels).astype(BF16)
            return carry

        lax.fori_loop(0, share // block, spread, 0)
        out[base + share * 2 * segs : base + height, :] = good.astype(BF16)


def whitened_parts(parts, me, taps, filtered, left, right, mask):
    segs, channels = mask.shape
    rows = NF // parts * 2 * segs + segs
    return pl.pallas_call(
        functools.partial(whiten_kernel, parts, taps.shape[0]),
        in_specs=[SCALARS] * 2 + [WHOLE] * 4,
        out_specs=[WHOLE] * 3,
        out_shape=[jax.ShapeDtypeStruct((height, channels), BF16) for height in (rows, rows, 2 * rows)],
        scratch_shapes=[
            pltpu.VMEM((2 * NF * segs, channels), F32),
            pltpu.VMEM((NF + 2 * SMOOTH, segs, channels), F32),
        ],
        compiler_params=pltpu.CompilerParams(vmem_limit_bytes=VMEM),
        name="whiten",
    )(me, taps, filtered, left, right, mask)


def pieces(arrays, height, first, size):
    rows = [
        ref[pl.ds(base + first, size), :]
        for ref in arrays
        for base in range(0, ref.shape[0], height)
    ]
    return jnp.concatenate(rows, axis=0)


def own_kernel(segs, bins, near, far, far_other, rows, sums, count):
    own = (near, far, far_other)
    height, channels = far.shape
    share = rows.shape[0]
    flags = pieces(own, height, height - segs, segs)
    count[...] = dot(flags, flags, TN)

    def group(step, carry):
        for at in range(bins):
            bin_at = step * bins + at
            first = pl.multiple_of(bin_at * (2 * segs), 2 * segs)
            mine = pieces(own, height, first, 2 * segs)
            split = mine.reshape(mine.shape[0] // (2 * segs), 2, segs, channels)
            turned = jnp.concatenate([-split[:, 1:], split[:, :1]], axis=1).reshape(mine.shape)
            both = jnp.concatenate([mine.T, turned.T], axis=0)
            rows[bin_at] = both
            sums[bin_at] = dot(both, mine)
        return carry

    lax.fori_loop(0, share // bins, group, 0)


def own_gram(parts, segs, near, far, far_other):
    channels = near.shape[1]
    share = NF // parts
    return pl.pallas_call(
        functools.partial(own_kernel, segs, 12),
        in_specs=[WHOLE] * 3,
        out_specs=[WHOLE] * 3,
        out_shape=[
            jax.ShapeDtypeStruct((share, 2 * channels, 2 * parts * segs), BF16),
            jax.ShapeDtypeStruct((share, 2 * channels, channels), F32),
            jax.ShapeDtypeStruct((channels, channels), F32),
        ],
        compiler_params=pltpu.CompilerParams(vmem_limit_bytes=VMEM),
        name="own_gram",
    )(near, far, far_other)


def gram_kernel(segs, batch, begin, first_half, *refs):
    if first_half:
        later_near, later_far, near, far, far_other, own_count, rows, sums, out, scale, cells, sems = refs
    else:
        later_near, later_far, scale, rows, sums, _, out, cells, sems = refs
    channels = later_near.shape[1]
    count = cells.shape[0]
    bins = count
    row = lax.broadcasted_iota(jnp.int32, (channels, channels), 0)
    column = lax.broadcasted_iota(jnp.int32, (channels, channels), 1)
    ahead = column > row
    skew = (row + column + 1) % channels
    near_height = count * 2 * segs
    far_height = later_far.shape[0] // 2

    def group_rows(ref, height, first, size):
        return [ref[pl.ds(base + first, size), :] for base in (0, height)]

    if first_half:
        height = far.shape[0]
        mine = pieces((near, far, far_other), height, height - segs, segs)
        theirs = jnp.concatenate(
            [later_near[2 * near_height :, :]]
            + group_rows(later_far, far_height, far_height - segs, segs),
            axis=0,
        )
        pairs = jnp.where(ahead, own_count[...], dot(mine, theirs, TN))
        scale[...] = 1.0 / jnp.maximum(pairs, 1.0)

    def group(step, carry):
        for at in range(bins):
            here = step * bins + at
            first = pl.multiple_of(here * (2 * segs), 2 * segs)
            theirs = jnp.concatenate(
                group_rows(later_near, near_height, first, 2 * segs)
                + group_rows(later_far, far_height, first + begin * 2 * segs, 2 * segs),
                axis=0,
            )
            gram = dot(rows[begin + here], theirs)
            for part in range(2):
                half = slice(part * channels, (part + 1) * channels)
                band = jnp.where(ahead, sums[begin + here, half, :], gram[half]) * scale[...]
                band = jnp.take_along_axis(band, skew, axis=1, mode="promise_in_bounds")
                cells[here, pl.ds(part, channels, stride=2), :] = band
            if at % batch == batch - 1:
                done = step * (bins // batch) + at // batch
                pltpu.make_async_copy(
                    cells.at[pl.ds(done * batch, batch)],
                    out.at[pl.ds(begin + done * batch, batch)],
                    sems.at[done],
                ).start()
        return carry

    lax.fori_loop(0, count // bins, group, 0)
    for done in range(count // batch):
        pltpu.make_async_copy(
            cells.at[pl.ds(done * batch, batch)],
            out.at[pl.ds(begin + done * batch, batch)],
            sems.at[done],
        ).wait()


def stacked(parts, segs, near, later_near, far, later_far):
    channels = near.shape[1]
    share = NF // parts
    batch = 2
    rows, sums, count = own_gram(parts, segs, near, *far)
    out = jax.ShapeDtypeStruct((share, 2 * channels, LAGS), F32)
    options = lambda bins: dict(
        scratch_shapes=[
            pltpu.VMEM((bins, 2 * channels, LAGS), F32),
            pltpu.SemaphoreType.DMA((bins // batch,)),
        ],
        compiler_params=pltpu.CompilerParams(vmem_limit_bytes=VMEM),
    )
    out, scale = pl.pallas_call(
        functools.partial(gram_kernel, segs, batch, 0, True),
        in_specs=[WHOLE] * 8,
        out_specs=[ANYWHERE, WHOLE],
        out_shape=[out, jax.ShapeDtypeStruct((channels, channels), F32)],
        name="gram",
        **options(CUTS[1]),
    )(later_near[0], later_far, near, *far, count, rows, sums)
    for at in range(1, len(CUTS) - 1):
        out = pl.pallas_call(
            functools.partial(gram_kernel, segs, batch, CUTS[at], False),
            in_specs=[WHOLE] * 5 + [ANYWHERE],
            out_specs=ANYWHERE,
            out_shape=jax.ShapeDtypeStruct(out.shape, F32),
            input_output_aliases={5: 0},
            name="gram_more",
            **options(CUTS[at + 1] - CUTS[at]),
        )(later_near[at], later_far, scale, rows, sums, out)
    return out


def on_device(fibers, parts, raw_strain, fir_taps, good_mask):
    segs, channels, samples = raw_strain.shape
    basis = basis_rows(samples)
    me = lax.axis_index("seg").astype(jnp.int32)
    head, tail = edge_spectra(basis, raw_strain)
    left = lax.ppermute(tail, "fiber", [(i, i + 1) for i in range(fibers - 1)])
    right = lax.ppermute(head, "fiber", [(i + 1, i) for i in range(fibers - 1)])
    filtered = main_spectra(basis, raw_strain, fir_taps)
    near, far, other = whitened_parts(
        parts, me[None], fir_taps, filtered, left, right, good_mask
    )
    rows = near.shape[0]
    swapped = lax.ppermute(other, "seg", [(j, j ^ 1) for j in range(parts)])
    across = [(j, j ^ 2) for j in range(parts)]
    own_far = [lax.ppermute(cells, "seg", across) for cells in (far, swapped[rows:])]
    near = jnp.concatenate([near, swapped[:rows]], axis=0)
    far = jnp.concatenate([far, swapped[rows:]], axis=0)

    def following(cells, flip):
        pairs = [
            ((i + 1) * parts + (j ^ flip), i * parts + j)
            for i in range(fibers - 1)
            for j in range(parts)
        ]
        return lax.ppermute(cells, GRID, pairs)

    later_far = following(far, 2)
    cut = lambda begin, stop: [near[begin:stop], near[rows + begin : rows + stop]]
    later_near = []
    for begin, stop in zip(CUTS, CUTS[1:]):
        cells = cut(begin * 2 * segs, stop * 2 * segs)
        if begin == 0:
            cells += cut(rows - segs, rows)
        later_near.append(following(jnp.concatenate(cells, axis=0), 0))
    out = stacked(parts, segs, near, later_near, own_far, later_far)
    return out.reshape(out.shape[0], channels, 2, LAGS)


def solution(mesh):
    return jax.shard_map(
        functools.partial(on_device, mesh.shape["fiber"], mesh.shape["seg"]),
        mesh=mesh,
        in_specs=(P("seg", "fiber", None), P(), P("seg", "fiber")),
        out_specs=P("seg", "fiber", None, None),
        check_vma=False,
    )
```
